512 devices in a mesh: seq: 64 (over y, z), head: 8 (over x, core).
Axes of the slice: x: 4, y: 4, z: 16, core: 2. Of those that a mesh axis runs over, the one named last changes fastest.
Arguments:
- queries: bfloat16 [65536, 2048], P(('seq', 'head')), may hold values from -6 to 6
- keys: bfloat16 [65536, 2048], P(('seq', 'head')), may hold values from -6 to 6
- values: bfloat16 [65536, 2048], P(('seq', 'head')), may hold values from -6 to 6
- cotangent: bfloat16 [65536, 2048], P(('seq', 'head')), may hold values from -6 to 6
- gain: float32 [2048], replicated, may hold values from 0.1 to 1.9
- lengths: int32 [32], replicated, may hold values from 1 to 16384, 65536 in all
Outputs:
- normed: bfloat16 [65536, 2048], P(('seq', 'head'))
- grad_queries: bfloat16 [65536, 2048], P('seq', 'head')
- grad_keys: bfloat16 [65536, 2048], P('seq', 'head')
- grad_values: bfloat16 [65536, 2048], P('seq', 'head')
The draws below stay inside these ranges and needn't reach their ends.
Inputs may be any that keep to these rules, and one draw needn't show every extreme that they name: The lengths sum to 65536, and the longest is exactly 16384.
All inputs are finite; a program needn't handle non-finite values.
Results may differ from the reference program's by a relative error of at most 0.012.
The reference program's roundings to bfloat16 on the way count: a program that leaves them out, or rounds other values in their place, can miss the bound.
Values may be sent and summed in bfloat16 or wider, within the bound.
No kernel may reach another device: no remote copies, remote signals or barrier semaphores. Data moves between devices by JAX's collectives and lax.ppermute only.
A program may use at most 64 MiB of HBM per device.

```python
import math
import jax
import jax.numpy as jnp
import numpy as np
from jax import lax

HEADS = 16
HEAD_DIM = 128
D = 2048
TOK_SEQ = 1024
TOKENS = 65536
DOCS = 32
MOST = 16384
N_SEQ = 64


def levels(key, extent, pieces, least, top_value):
    level = 1.0
    for dim, blocks in pieces:
        steps = jax.random.uniform(jax.random.fold_in(jax.random.fold_in(key, 6), dim), (blocks,), jnp.float32, least / len(pieces), top_value / len(pieces))
        level = level * jnp.repeat(jnp.exp(steps), extent[dim] // blocks).reshape((-1,) + (1,) * (len(extent) - 1 - dim))
    return level


def split_up(count, total, limit, skew):
    loads = [(1 << 20) // math.isqrt(grade ** skew) + 1 for grade in range(2, count + 1)]
    rest, holding = total - limit - (count - 1), [1] * (count - 1)
    while rest > 0:
        free = [i for i in range(count - 1) if holding[i] < limit]
        whole, left = sum([loads[i] for i in free]), rest
        for i in free:
            addition = min(limit - holding[i], max(1, left * loads[i] // whole), rest)
            holding[i] = holding[i] + addition
            rest = rest - addition
    return np.array([limit] + holding)


def uneven(own_key, amount, total, most, skew):
    if amount == 2:
        one = jax.random.randint(own_key, (), max(1, total - most), min(most, total - 1) + 1)
        return jnp.stack([one, total - one])
    tallies = jnp.asarray(split_up(amount, total, most, skew), jnp.int32)
    twos = (amount - 1) // 2
    donor, receiver = tallies[1:1 + 2 * twos:2], tallies[2:2 + 2 * twos:2]
    slack = jnp.minimum(donor - 1, most - receiver)
    moved = jax.random.randint(jax.random.fold_in(own_key, 1), (twos,), 0, 1 << 20) % (slack + 1)
    tallies = tallies.at[1:1 + 2 * twos:2].set(donor - moved).at[2:2 + 2 * twos:2].set(receiver + moved)
    return tallies[jax.random.permutation(jax.random.fold_in(own_key, 2), amount)]


def noise(own_key, extent, spread, most, pieces=(), held_as=jnp.bfloat16):
    loudness = levels(own_key, extent, pieces, -0.22, 0.18) if pieces else 1.0
    entries = jax.random.normal(own_key, extent, jnp.float32) * spread * loudness
    return jnp.minimum(jnp.maximum(entries, -most), most).astype(held_as)


def setup_inputs(seed: int = 0) -> dict:
    seeds = jax.random.split(jax.random.key(seed), 7)
    queries = noise(seeds[0], (TOKENS, D), 1.0, 6.0, ((0, 512),))
    keys = noise(seeds[1], (TOKENS, D), 1.0, 6.0, ((0, 512),))
    values = noise(seeds[2], (TOKENS, D), 1.0, 6.0, ((0, 512),))
    cotangent = noise(seeds[3], (TOKENS, D), 1.0, 6.0, ((0, 512),))
    gain = jnp.clip(1.0 + 0.18 * jax.random.normal(seeds[4], (D,), jnp.float32), 0.1, 1.9)
    lengths = uneven(seeds[5], DOCS, TOKENS, MOST, 2).astype(jnp.int32)
    return dict(queries=queries, keys=keys, values=values, cotangent=cotangent, gain=gain, lengths=lengths)


epsilon = 1e-05

def doc_index(positions, starts):
    hits = (positions[:, None] >= starts[None, :]).astype(jnp.int32)
    return (lax.optimization_barrier(jnp.sum(hits, axis=1)) - 1).astype(jnp.int32)

def normalize(field, gain_heads):
    mean_square = lax.optimization_barrier(jnp.mean(field * field, axis=-1, keepdims=True))
    return field * lax.rsqrt(mean_square + epsilon) * gain_heads

def rounded(field):
    return lax.optimization_barrier(field.astype(jnp.bfloat16)).astype(jnp.float32)

def block_mask(doc_block):
    places = jnp.arange(TOK_SEQ, dtype=jnp.int32)
    causal = places[:, None] >= places[None, :]
    return causal & (doc_block[:, None] == doc_block[None, :])

def reference(queries, keys, values, cotangent, gain, lengths):
    starts = (jnp.cumsum(lengths) - lengths).astype(jnp.int32)
    docs = doc_index(jnp.arange(TOKENS, dtype=jnp.int32), starts).reshape(N_SEQ, TOK_SEQ)
    prev_docs = jnp.concatenate([jnp.full((1,), -1, jnp.int32), docs[:-1, -1]])
    next_docs = jnp.concatenate([docs[1:, 0], docs[-1:, -1]])
    shape = (N_SEQ, TOK_SEQ, HEADS, HEAD_DIM)
    q_all = queries.reshape(shape)
    k_all = keys.reshape(shape)
    v_all = values.reshape(shape)
    g_all = cotangent.reshape(shape)
    gain_heads = gain.reshape(HEADS, HEAD_DIM).astype(jnp.float32)

    def forward_step(state, block):
        q_b, k_b, v_b, g_b, doc_b, prev = block
        qf = q_b.astype(jnp.float32)
        kf = k_b.astype(jnp.float32)
        vf = v_b.astype(jnp.float32)
        mask = block_mask(doc_b)
        scores = jnp.einsum('thd,shd->hts', qf, kf)
        attn = rounded(jnp.where(mask[None], scores, 0.0))
        intra = jnp.einsum('hts,she->the', attn, vf)
        state_low = rounded(state)
        carried = (doc_b == prev)[:, None, None]
        inter = jnp.einsum('thd,hde->the', qf, state_low)
        attended = intra + jnp.where(carried, inter, 0.0)
        normed_b = normalize(attended, gain_heads).astype(jnp.bfloat16)
        _, pullback = jax.vjp(lambda field: normalize(field, gain_heads), attended)
        grad_att = pullback(g_b.astype(jnp.float32))[0].astype(jnp.bfloat16)
        last = doc_b[-1]
        tail_keys = jnp.where((doc_b == last)[:, None, None], kf, 0.0)
        tail = jnp.einsum('thd,the->hde', tail_keys, vf)
        new_state = jnp.where(last != prev, tail, state + tail)
        return (new_state, (state, normed_b, grad_att))
    zero_state = jnp.zeros((HEADS, HEAD_DIM, HEAD_DIM), jnp.float32)
    _, (states, normed_all, grad_all) = lax.scan(forward_step, zero_state, (q_all, k_all, v_all, g_all, docs, prev_docs))

    def backward_step(back, block):
        q_b, k_b, v_b, d_b, state, doc_b, prev, nxt = block
        qf = q_b.astype(jnp.float32)
        kf = k_b.astype(jnp.float32)
        vf = v_b.astype(jnp.float32)
        df = d_b.astype(jnp.float32)
        mask = block_mask(doc_b)
        attn = rounded(jnp.where(mask[None], jnp.einsum('thd,shd->hts', qf, kf), 0.0))
        grad_attn = rounded(jnp.where(mask[None], jnp.einsum('the,she->hts', df, vf), 0.0))
        state_low = rounded(state)
        back_low = rounded(back)
        carried = (doc_b == prev)[:, None, None]
        later = (doc_b == nxt)[:, None, None]
        grad_q = jnp.einsum('hts,shd->thd', grad_attn, kf) + jnp.where(carried, jnp.einsum('the,hde->thd', df, state_low), 0.0)
        grad_k = jnp.einsum('hts,thd->shd', grad_attn, qf) + jnp.where(later, jnp.einsum('she,hde->shd', vf, back_low), 0.0)
        grad_v = jnp.einsum('hts,the->she', attn, df) + jnp.where(later, jnp.einsum('shd,hde->she', kf, back_low), 0.0)
        first = doc_b[0]
        head_queries = jnp.where((doc_b == first)[:, None, None], qf, 0.0)
        head_part = jnp.einsum('thd,the->hde', head_queries, df)
        new_back = jnp.where(first != nxt, head_part, back + head_part)
        outs = (grad_q.astype(jnp.bfloat16), grad_k.astype(jnp.bfloat16), grad_v.astype(jnp.bfloat16))
        return (new_back, outs)
    _, (grad_q_all, grad_k_all, grad_v_all) = lax.scan(backward_step, zero_state, (q_all, k_all, v_all, grad_all, states, docs, prev_docs, next_docs), reverse=True)
    flat = (TOKENS, D)
    return (normed_all.reshape(flat), grad_q_all.reshape(flat), grad_k_all.reshape(flat), grad_v_all.reshape(flat))
```

```python
import functools

import jax
import jax.numpy as jnp
from jax import lax
from jax.experimental import pallas as pl
from jax.experimental.pallas import tpu as pltpu
from jax.sharding import PartitionSpec as P

HEAD_DIM = 128
TILE = 256
SPAN = 4
SPANS = 4
epsilon = 1e-05

F32 = jnp.float32
BF16 = jnp.bfloat16

ROWS = (((0,), (0,)), ((), ()))
FEATURES = (((1,), (1,)), ((), ()))
PLAIN = (((1,), (0,)), ((), ()))


def dot(a, b, dims):
    return lax.dot_general(a, b, dims, preferred_element_type=F32)


def unpacked(packed_ref, at):
    groups, stacked, width = packed_ref.shape
    tokens = stacked // 4
    return packed_ref[:, at * tokens : (at + 1) * tokens, :].reshape(groups * tokens, width)


def head_cols(head):
    return slice(head * HEAD_DIM, (head + 1) * HEAD_DIM)


def meta_kernel(blocks, rows, lengths_ref, where_ref, marks_ref):
    first = where_ref[0] * rows
    last = first + rows - 1

    def clear(i, carry):
        marks_ref[i] = 0
        return carry

    lax.fori_loop(0, 2 * blocks, clear, 0)
    marks_ref[2 * blocks - 1] = 1
    marks_ref[2 * blocks + 1] = 0
    marks_ref[2 * blocks + 3] = rows

    def step(i, begin):
        after = begin + lengths_ref[i]
        marks_ref[begin // rows] = 1
        marks_ref[blocks + jnp.maximum(begin - 1, 0) // rows] = 1

        @pl.when((begin <= first) & (first < after))
        def _():
            marks_ref[2 * blocks] = after - first
            marks_ref[2 * blocks + 1] = jnp.where(begin < first, after - first, 0)

        @pl.when((begin <= last) & (last < after))
        def _():
            marks_ref[2 * blocks + 2] = begin - first
            marks_ref[2 * blocks + 3] = jnp.where(after > last + 1, begin - first, rows)

        return after

    lax.fori_loop(0, lengths_ref.shape[0], step, jnp.int32(0))


def docs_kernel(lengths_ref, where_ref, span_ref):
    rows = span_ref.shape[1]
    first = where_ref[0] * rows
    place = first + lax.broadcasted_iota(jnp.int32, (1, rows), 1)

    def step(i, carry):
        begin, start, end = carry
        after = begin + lengths_ref[i]
        inside = (place >= begin) & (place < after)
        return (after, jnp.where(inside, begin, start), jnp.where(inside, after, end))

    zero = jnp.zeros((1, rows), jnp.int32)
    _, start, end = lax.fori_loop(0, lengths_ref.shape[0], step, (jnp.int32(0), zero, zero))
    span_ref[0:1, :] = start - first
    span_ref[1:2, :] = end - first


def pack_kernel(*refs):
    *arrays, ended_ref, out_ref, held, in_sems, out_sems = refs
    ended_ref[...] = jnp.zeros_like(ended_ref)
    groups, _, width = out_ref.shape
    tokens = arrays[0].shape[0]
    inward = [
        pltpu.make_async_copy(ref, held.at[k], in_sems.at[k]) for k, ref in enumerate(arrays)
    ]
    outward = [
        [
            pltpu.make_async_copy(
                held.at[k, :, pl.ds(at * width, width)],
                out_ref.at[at, pl.ds(k * tokens, tokens), :],
                out_sems.at[k, at],
            )
            for at in range(groups)
        ]
        for k in range(len(arrays))
    ]
    for copy in inward:
        copy.start()
    for copy, parts in zip(inward, outward):
        copy.wait()
        for part in parts:
            part.start()
    for parts in outward:
        for part in parts:
            part.wait()


def parts_kernel(lengths_ref, where_ref, keys_ref, values_ref, ended_ref, out_ref, held, sems):
    copies = [
        pltpu.make_async_copy(ref, held.at[k], sems.at[k])
        for k, ref in enumerate((keys_ref, values_ref))
    ]
    for copy in copies:
        copy.start()
    ended_ref[...] = jnp.zeros_like(ended_ref)
    groups, width, _ = out_ref.shape
    tokens, cols = keys_ref.shape
    last = (where_ref[0] + 1) * (tokens * groups) - 1
    begin, bound = jnp.int32(0), jnp.int32(0)
    for i in range(lengths_ref.shape[0]):
        bound = jnp.where(begin <= last, begin, bound)
        begin = begin + lengths_ref[i]
    mine = last + 1 - (groups - where_ref[1]) * tokens
    for copy in copies:
        copy.wait()
    place = mine + lax.broadcasted_iota(jnp.int32, (tokens, cols), 0)
    keys = held[0]
    keys = jnp.where(place >= bound, keys, jnp.zeros_like(keys))
    for head in range(cols // HEAD_DIM):
        part = dot(keys[:, head_cols(head)], held[1, :, head_cols(head)], ROWS)
        group, at = divmod(head * HEAD_DIM, width)
        out_ref[group, at : at + HEAD_DIM, :] = part.astype(out_ref.dtype)


def tail_kernel(marks_ref, parts_ref, tail_ref):
    total = parts_ref[0].astype(F32)
    for k in range(1, parts_ref.shape[0]):
        total = total + parts_ref[k].astype(F32)
    tail_ref[...] = total.astype(tail_ref.dtype)


def scan_kernel(reverse, marks_ref, parts_ref, low_ref):
    blocks = parts_ref.shape[0]
    total = jnp.zeros(parts_ref.shape[1:], F32)
    for k in range(blocks):
        at = blocks - 1 - k if reverse else k
        low_ref[at] = total.astype(low_ref.dtype)
        part = parts_ref[at].astype(F32)
        mark = marks_ref[at + (blocks if reverse else 0)]
        total = jnp.where(mark > 0, part, total + part)


def block_mark(marks_ref, blocks, at, reverse):
    return marks_ref[lax.rem(at + blocks, blocks) + (blocks if reverse else 0)]


def span_kernel(reverse, blocks, where_ref, marks_ref, *refs):
    span_ref = refs[-1]
    mine, sign = where_ref[0], -1 if reverse else 1
    total = refs[0][...].astype(F32)
    for k, ref in enumerate(refs[1:-1]):
        mark = block_mark(marks_ref, blocks, mine + sign * (k - 1), reverse)
        total = jnp.where(mark > 0, 0.0, total) + ref[...].astype(F32)
    span_ref[...] = total.astype(span_ref.dtype)


def entering(reverse, blocks, where_ref, marks_ref, span_refs):
    mine, sign = where_ref[0], -1 if reverse else 1
    total = span_refs[0][...].astype(F32)
    for k, ref in enumerate(span_refs[1:]):
        first = SPAN * (SPANS - 1 - k)
        mark = jnp.int32(0)
        for back in range(first - SPAN + 1, first + 1):
            mark = jnp.maximum(mark, block_mark(marks_ref, blocks, mine - sign * back, reverse))
        total = jnp.where(mark > 0, 0.0, total) + ref[...].astype(F32)
    return total.astype(BF16)


def intra_kernel(span_ref, packed_ref, intra_ref):
    keys, values, queries = (unpacked(packed_ref, at) for at in range(3))
    rows, width = keys.shape
    for low in range(0, rows, TILE):
        high = low + TILE
        row = low + lax.broadcasted_iota(jnp.int32, (TILE, high), 0)
        column = lax.broadcasted_iota(jnp.int32, (TILE, high), 1)
        mask = (column <= row) & (row < span_ref[1:2, :high])
        for head in range(width // HEAD_DIM):
            cols = head_cols(head)
            scores = dot(queries[low:high, cols], keys[:high, cols], FEATURES)
            attn = jnp.where(mask, scores, 0.0).astype(BF16)
            intra_ref[low:high, cols] = dot(attn, values[:high, cols], PLAIN)


def norm_kernel(blocks, where_ref, marks_ref, packed_ref, intra_ref, gain_ref, *refs):
    span_refs, (normed_ref, grad_ref, part_ref, state_ref) = refs[:SPANS], refs[SPANS:]
    queries, cotangent = unpacked(packed_ref, 2), unpacked(packed_ref, 3)
    state = entering(False, blocks, where_ref, marks_ref, span_refs)
    state_ref[...] = state
    rows, width = intra_ref.shape
    place = lax.broadcasted_iota(jnp.int32, (rows, HEAD_DIM), 0)
    in_first = place < marks_ref[2 * blocks]
    carried = place < marks_ref[2 * blocks + 1]
    for head in range(width // HEAD_DIM):
        cols = head_cols(head)
        q = queries[:, cols]
        inter = dot(q, state[cols, :], PLAIN)
        attended = intra_ref[:, cols] + jnp.where(carried, inter, 0.0)
        at = pl.multiple_of(where_ref[1] * width + head * HEAD_DIM, HEAD_DIM)
        gain = gain_ref[:, pl.ds(at, HEAD_DIM)]
        scale = lax.rsqrt(jnp.mean(attended * attended, axis=-1, keepdims=True) + epsilon)
        unit = attended * scale
        normed_ref[:, cols] = (unit * gain).astype(BF16)
        pulled = cotangent[:, cols].astype(F32) * gain
        along = jnp.mean(pulled * unit, axis=-1, keepdims=True)
        grad = (scale * (pulled - unit * along)).astype(BF16)
        grad_ref[:, cols] = grad
        kept = jnp.where(in_first, q, jnp.zeros_like(q))
        part_ref[cols, :] = dot(kept, grad, ROWS).astype(part_ref.dtype)


def grad_q_kernel(blocks, marks_ref, span_ref, packed_ref, grad_ref, state_ref, ended_ref, grad_q_ref):
    ended_ref[...] = jnp.zeros_like(ended_ref)
    keys, values = unpacked(packed_ref, 0), unpacked(packed_ref, 1)
    rows, width = keys.shape
    for low in range(0, rows, TILE):
        high = low + TILE
        row = low + lax.broadcasted_iota(jnp.int32, (TILE, high), 0)
        column = lax.broadcasted_iota(jnp.int32, (TILE, high), 1)
        mask = (column <= row) & (row < span_ref[1:2, :high])
        place = low + lax.broadcasted_iota(jnp.int32, (TILE, HEAD_DIM), 0)
        carried = place < marks_ref[2 * blocks + 1]
        for head in range(width // HEAD_DIM):
            cols = head_cols(head)
            grad = grad_ref[low:high, cols]
            scores = dot(grad, values[:high, cols], FEATURES)
            grad_attn = jnp.where(mask, scores, 0.0).astype(BF16)
            inter = dot(grad, state_ref[cols, :], FEATURES)
            grad_q = dot(grad_attn, keys[:high, cols], PLAIN) + jnp.where(carried, inter, 0.0)
            grad_q_ref[low:high, cols] = grad_q.astype(BF16)


def grad_kv_kernel(span_ref, packed_ref, grad_ref, part_k_ref, part_v_ref):
    keys, values, queries = (unpacked(packed_ref, at) for at in range(3))
    rows, width = keys.shape
    for low in range(0, rows, TILE):
        high = low + TILE
        row = low + lax.broadcasted_iota(jnp.int32, (TILE, rows - low), 0)
        column = low + lax.broadcasted_iota(jnp.int32, (TILE, rows - low), 1)
        mask = (row <= column) & (row >= span_ref[0:1, low:])
        for head in range(width // HEAD_DIM):
            cols = head_cols(head)
            q, k, v = (field[:, cols] for field in (queries, keys, values))
            grad = grad_ref[:, cols]
            turned = dot(v[low:high], grad[low:], FEATURES)
            turned = jnp.where(mask, turned, 0.0).astype(BF16)
            part_k_ref[low:high, cols] = dot(turned, q[low:], PLAIN)
            turned = dot(k[low:high], q[low:], FEATURES)
            turned = jnp.where(mask, turned, 0.0).astype(BF16)
            part_v_ref[low:high, cols] = dot(turned, grad[low:], PLAIN)


def last_kernel(blocks, marks_ref, packed_ref, part_k_ref, part_v_ref, back_ref, grad_k_ref, grad_v_ref):
    keys, values = unpacked(packed_ref, 0), unpacked(packed_ref, 1)
    rows, width = keys.shape
    place = lax.broadcasted_iota(jnp.int32, (rows, HEAD_DIM), 0)
    later = place >= marks_ref[2 * blocks + 3]
    for head in range(width // HEAD_DIM):
        cols = head_cols(head)
        inter = dot(values[:, cols], back_ref[cols, :], FEATURES)
        grad_k_ref[:, cols] = (part_k_ref[:, cols] + jnp.where(later, inter, 0.0)).astype(BF16)
        inter = dot(keys[:, cols], back_ref[cols, :], PLAIN)
        grad_v_ref[:, cols] = (part_v_ref[:, cols] + jnp.where(later, inter, 0.0)).astype(BF16)


SMEM = pl.BlockSpec(memory_space=pltpu.SMEM)
VMEM = pl.BlockSpec(memory_space=pltpu.VMEM)
ANYWHERE = pl.BlockSpec(memory_space=pl.ANY)
ENDED = jax.ShapeDtypeStruct((8, HEAD_DIM), F32)


def call(
    kernel, name, outs, scalars, arrays, flops, scratch=(), after=(), in_specs=None, out_specs=None, limit=40, aliases=None
):
    moved = sum(a.size * a.dtype.itemsize for a in (*arrays, *outs))
    given = len(scalars) + len(arrays)

    def body(*refs):
        kernel(*refs[:given], *refs[given + len(after) :])

    return pl.pallas_call(
        body,
        name=name,
        out_shape=outs,
        in_specs=[SMEM] * len(scalars) + (in_specs or [VMEM] * len(arrays)) + [ANYWHERE] * len(after),
        out_specs=out_specs or [VMEM] * len(outs),
        scratch_shapes=list(scratch),
        input_output_aliases=aliases or {},
        compiler_params=pltpu.CompilerParams(vmem_limit_bytes=limit * 1024 * 1024),
        cost_estimate=pl.CostEstimate(flops=flops, bytes_accessed=moved, transcendentals=0),
    )(*scalars, *arrays, *after)


def across_head(parts):
    return lax.all_to_all(parts, "head", split_axis=0, concat_axis=0, tiled=True)


def to_heads(arrays, after):
    groups, count = lax.axis_size("head"), len(arrays)
    tokens, cols = arrays[0].shape
    ended, packed = call(
        pack_kernel,
        "pack",
        [ENDED, jax.ShapeDtypeStruct((groups, count * tokens, cols // groups), BF16)],
        [],
        arrays,
        0,
        [
            pltpu.VMEM((count, tokens, cols), BF16),
            pltpu.SemaphoreType.DMA((count,)),
            pltpu.SemaphoreType.DMA((count, groups)),
        ],
        after,
        [ANYWHERE] * count,
        [VMEM, ANYWHERE],
        60,
    )
    return ended, across_head(packed)


def from_block(field, step):
    blocks = lax.axis_size("seq")
    return lax.ppermute(field, "seq", [(at, (at + step) % blocks) for at in range(blocks)])


def spans_before(part, where, marks, reverse):
    sign = -1 if reverse else 1
    parts = [from_block(part, sign * 2), from_block(part, sign), part, from_block(part, -sign)]
    (span,) = call(
        functools.partial(span_kernel, reverse, lax.axis_size("seq")),
        "span_back" if reverse else "span_forward",
        [jax.ShapeDtypeStruct(part.shape, BF16)],
        [where, marks],
        parts,
        SPAN * part.size,
    )
    spans = {k: from_block(span, sign * (2 + SPAN * k)) for k in (2, 1, 3, 0)}
    return [spans[k] for k in reversed(range(SPANS))], parts[0]


def carried_over(part, marks, reverse, beside):
    blocks = lax.axis_size("seq")
    height, width = part.shape
    first = beside[0]([part])
    sent = part.reshape(blocks, height // blocks, width)
    got = lax.all_to_all(sent, "seq", split_axis=0, concat_axis=0, tiled=True)
    (low,) = call(
        functools.partial(scan_kernel, reverse),
        "scan_back" if reverse else "scan_forward",
        [jax.ShapeDtypeStruct(got.shape, BF16)],
        [marks],
        [got],
        got.size,
        after=first[:1],
    )
    second = beside[1]([low], first)
    mine = lax.all_to_all(low, "seq", split_axis=0, concat_axis=0, tiled=True)
    return mine.reshape(height, width), first, second


def on_device(queries, keys, values, cotangent, gain, lengths):
    groups, blocks = lax.axis_size("head"), lax.axis_size("seq")
    tokens, cols = queries.shape
    rows, width = tokens * groups, cols // groups
    square = rows * rows * width
    here = lax.axis_index("head").astype(jnp.int32)
    where = jnp.stack([lax.axis_index("seq").astype(jnp.int32), here])
    f32 = functools.partial(jax.ShapeDtypeStruct, dtype=F32)
    bf16 = functools.partial(jax.ShapeDtypeStruct, dtype=BF16)
    int32 = functools.partial(jax.ShapeDtypeStruct, dtype=jnp.int32)
    started, parts = call(
        parts_kernel,
        "parts",
        [ENDED, bf16((groups, width, HEAD_DIM))],
        [lengths, where],
        [keys, values],
        2 * tokens * cols * HEAD_DIM,
        [pltpu.VMEM((2, tokens, cols), BF16), pltpu.SemaphoreType.DMA((2,))],
        in_specs=[ANYWHERE] * 2,
        limit=60,
    )
    (marks,) = call(
        functools.partial(meta_kernel, blocks, rows),
        "meta",
        [int32((2 * blocks + 4,))],
        [lengths, where],
        [],
        rows,
        after=[started],
        out_specs=[SMEM],
    )
    (span,) = call(docs_kernel, "docs", [int32((2, rows))], [lengths, where], [], rows, after=[started])
    gathered = across_head(parts)
    ended, packed = to_heads([keys, values, queries, cotangent], [started])
    (tail,) = call(
        tail_kernel,
        "tail",
        [bf16((width, HEAD_DIM))],
        [marks],
        [gathered],
        gathered.size,
        after=[ended, span],
    )
    before, _ = spans_before(tail, where, marks, False)
    (inside,) = call(intra_kernel, "intra", [f32((rows, width))], [], [span, packed], 2 * square)
    normed, grad, part, state = call(
        functools.partial(norm_kernel, blocks),
        "norm",
        [bf16((rows, width)), bf16((rows, width)), bf16((width, HEAD_DIM)), bf16((width, HEAD_DIM))],
        [where, marks],
        [packed, inside, gain.reshape(1, cols), *before],
        4 * rows * width * HEAD_DIM,
    )

    def grads_q(after):
        return call(
            functools.partial(grad_q_kernel, blocks),
            "grads_q",
            [ENDED, bf16((rows, width))],
            [marks],
            [span, packed, grad, state],
            2 * square,
            after=after,
        )

    def grads_kv(after, _):
        return call(
            grad_kv_kernel,
            "grads_kv",
            [f32((rows, width)), f32((rows, width))],
            [],
            [span, packed, grad],
            4 * square,
            after=after,
        )

    back, (_, grad_q), (part_k, part_v) = carried_over(part, marks, True, (grads_q, grads_kv))
    (normed,) = call(
        lambda *refs: None,
        "normed",
        [bf16((rows, width))],
        [],
        [normed],
        0,
        after=[back],
        in_specs=[ANYWHERE],
        out_specs=[ANYWHERE],
        aliases={0: 0},
    )
    normed = across_head(normed.reshape(groups, tokens, width))
    grad_k, grad_v = call(
        functools.partial(last_kernel, blocks),
        "last",
        [bf16((rows, width)), bf16((rows, width))],
        [marks],
        [packed, part_k, part_v, back],
        4 * rows * width * HEAD_DIM,
    )
    return normed.transpose(1, 0, 2).reshape(tokens, cols), grad_q, grad_k, grad_v


def solution(mesh):
    placed = P(("seq", "head"), None)
    return jax.shard_map(
        on_device,
        mesh=mesh,
        in_specs=(placed, placed, placed, placed, P(), P()),
        out_specs=(placed, P("seq", "head"), P("seq", "head"), P("seq", "head")),
        check_vma=False,
    )
```

```python
import functools

import jax
import jax.numpy as jnp
from jax import lax
from jax.experimental import pallas as pl
from jax.experimental.pallas import tpu as pltpu
from jax.sharding import PartitionSpec as P

HEAD_DIM = 128
TILE = 256


epsilon = 1e-05

F32 = jnp.float32
BF16 = jnp.bfloat16

ROWS = (((0,), (0,)), ((), ()))
FEATURES = (((1,), (1,)), ((), ()))
PLAIN = (((1,), (0,)), ((), ()))


def dot(a, b, dims):
    return lax.dot_general(a, b, dims, preferred_element_type=F32)


def unpacked(packed_ref, at):
    groups, stacked, width = packed_ref.shape
    tokens = stacked // 4
    return packed_ref[:, at * tokens : (at + 1) * tokens, :].reshape(groups * tokens, width)


def head_cols(head):
    return slice(head * HEAD_DIM, (head + 1) * HEAD_DIM)


def meta_kernel(blocks, rows, lengths_ref, where_ref, marks_ref):
    first = where_ref[0] * rows
    last = first + rows - 1

    def clear(i, carry):
        marks_ref[i] = 0
        return carry

    lax.fori_loop(0, 2 * blocks, clear, 0)
    marks_ref[2 * blocks - 1] = 1
    marks_ref[2 * blocks + 1] = 0
    marks_ref[2 * blocks + 3] = rows

    def step(i, begin):
        after = begin + lengths_ref[i]
        marks_ref[begin // rows] = 1
        marks_ref[blocks + jnp.maximum(begin - 1, 0) // rows] = 1

        @pl.when((begin <= first) & (first < after))
        def _():
            marks_ref[2 * blocks] = after - first
            marks_ref[2 * blocks + 1] = jnp.where(begin < first, after - first, 0)

        @pl.when((begin <= last) & (last < after))
        def _():
            marks_ref[2 * blocks + 2] = begin - first
            marks_ref[2 * blocks + 3] = jnp.where(after > last + 1, begin - first, rows)

        return after

    lax.fori_loop(0, lengths_ref.shape[0], step, jnp.int32(0))


def docs_kernel(lengths_ref, where_ref, marks_ref, span_ref):
    rows = span_ref.shape[1]
    first = where_ref[0] * rows
    place = first + lax.broadcasted_iota(jnp.int32, (1, rows), 1)

    def step(i, carry):
        begin, start, end = carry
        after = begin + lengths_ref[i]
        inside = (place >= begin) & (place < after)
        return (after, jnp.where(inside, begin, start), jnp.where(inside, after, end))

    zero = jnp.zeros((1, rows), jnp.int32)
    _, start, end = lax.fori_loop(0, lengths_ref.shape[0], step, (jnp.int32(0), zero, zero))
    span_ref[0:1, :] = start - first
    span_ref[1:2, :] = end - first


def pack_kernel(*refs):
    *arrays, ended_ref, out_ref, held, in_sems, out_sems = refs
    ended_ref[...] = jnp.zeros_like(ended_ref)
    groups, _, width = out_ref.shape
    tokens = arrays[0].shape[0]
    inward = [
        pltpu.make_async_copy(ref, held.at[k], in_sems.at[k]) for k, ref in enumerate(arrays)
    ]
    outward = [
        [
            pltpu.make_async_copy(
                held.at[k, :, pl.ds(at * width, width)],
                out_ref.at[at, pl.ds(k * tokens, tokens), :],
                out_sems.at[k, at],
            )
            for at in range(groups)
        ]
        for k in range(len(arrays))
    ]
    for copy in inward:
        copy.start()
    for copy, parts in zip(inward, outward):
        copy.wait()
        for part in parts:
            part.start()
    for parts in outward:
        for part in parts:
            part.wait()


def parts_kernel(
    lengths_ref, seq_ref, head_ref, keys_ref, values_ref, ended_ref, out_ref, held, sums, in_sems, out_sems
):
    inward = [
        pltpu.make_async_copy(ref, held.at[k], in_sems.at[k])
        for k, ref in enumerate((keys_ref, values_ref))
    ]
    for copy in inward:
        copy.start()
    ended_ref[...] = jnp.zeros_like(ended_ref)
    groups, width, _ = out_ref.shape
    tokens, cols = keys_ref.shape
    last = (seq_ref[0] + 1) * (tokens * groups) - 1
    begin, bound = jnp.int32(0), jnp.int32(0)
    for i in range(lengths_ref.shape[0]):
        bound = jnp.where(begin <= last, begin, bound)
        begin = begin + lengths_ref[i]
    mine = last + 1 - (groups - head_ref[0]) * tokens
    place = mine + lax.broadcasted_iota(jnp.int32, (tokens, HEAD_DIM), 0)
    for copy in inward:
        copy.wait()
    outward = []
    for group in range(groups):
        for head in range(width // HEAD_DIM):
            at = slice(group * width + head * HEAD_DIM, group * width + (head + 1) * HEAD_DIM)
            keys = held[0, :, at]
            keys = jnp.where(place >= bound, keys, jnp.zeros_like(keys))
            part = dot(keys, held[1, :, at], ROWS)
            sums[group, head_cols(head), :] = part.astype(sums.dtype)
        copy = pltpu.make_async_copy(sums.at[group], out_ref.at[group], out_sems.at[group])
        copy.start()
        outward.append(copy)
    for copy in outward:
        copy.wait()


def tail_kernel(marks_ref, parts_ref, tail_ref):
    total = parts_ref[0].astype(F32)
    for k in range(1, parts_ref.shape[0]):
        total = total + parts_ref[k].astype(F32)
    tail_ref[...] = total.astype(tail_ref.dtype)


def block_mark(marks_ref, blocks, at, reverse):
    return marks_ref[lax.rem(at + blocks, blocks) + (blocks if reverse else 0)]


def chained(reverse, blocks, where_ref, marks_ref, refs, covers):
    mine, sign = where_ref[0], -1 if reverse else 1
    total = refs[0][...].astype(F32)
    for ref, (low, high) in zip(refs[1:], covers[1:]):
        mark = jnp.int32(0)
        for at in range(low, high + 1):
            mark = jnp.maximum(mark, block_mark(marks_ref, blocks, mine + sign * at, reverse))
        total = jnp.where(mark > 0, 0.0, total) + ref[...].astype(F32)
    return total.astype(BF16)


def three_kernel(reverse, blocks, where_ref, marks_ref, *refs):
    *parts, span_ref = refs
    covers = ((-1, -1), (0, 0), (1, 1))
    span_ref[...] = chained(reverse, blocks, where_ref, marks_ref, parts, covers)


def nine_kernel(reverse, blocks, where_ref, marks_ref, *refs):
    *parts, span_ref = refs
    covers = ((-4, -2), (-1, 1), (2, 4))
    span_ref[...] = chained(reverse, blocks, where_ref, marks_ref, parts, covers)


def entering(reverse, blocks, where_ref, marks_ref, *refs):
    return chained(reverse, blocks, where_ref, marks_ref, refs, ((-18, -10), (-9, -1)))


def intra_kernel(span_ref, packed_ref, intra_ref):
    keys, values, queries = (unpacked(packed_ref, at) for at in range(3))
    rows, width = keys.shape
    for low in range(0, rows, TILE):
        high = low + TILE
        row = low + lax.broadcasted_iota(jnp.int32, (TILE, high), 0)
        column = lax.broadcasted_iota(jnp.int32, (TILE, high), 1)
        mask = (column <= row) & (row < span_ref[1:2, :high])
        for head in range(width // HEAD_DIM):
            cols = head_cols(head)
            scores = dot(queries[low:high, cols], keys[:high, cols], FEATURES)
            attn = jnp.where(mask, scores, 0.0).astype(BF16)
            intra_ref[low:high, cols] = dot(attn, values[:high, cols], PLAIN)


def norm_kernel(blocks, where_ref, marks_ref, packed_ref, intra_ref, gain_ref, *refs):
    far_ref, near_ref, normed_ref, grad_ref, part_ref, state_ref, held, sems = refs
    queries, cotangent = unpacked(packed_ref, 2), unpacked(packed_ref, 3)
    state = entering(False, blocks, where_ref, marks_ref, far_ref, near_ref)
    state_ref[...] = state
    rows, width = intra_ref.shape
    tile = HEAD_DIM
    outward = []
    for low in range(0, rows, tile):
        here = slice(low, low + tile)
        place = low + lax.broadcasted_iota(jnp.int32, (tile, HEAD_DIM), 0)
        for head in range(width // HEAD_DIM):
            cols = head_cols(head)
            at = pl.multiple_of(where_ref[1] * width + head * HEAD_DIM, HEAD_DIM)
            gain = gain_ref[:, pl.ds(at, HEAD_DIM)]
            inter = dot(queries[here, cols], state[cols, :], PLAIN)
            inter = jnp.where(place < marks_ref[2 * blocks + 1], inter, 0.0)
            attended = intra_ref[here, cols] + inter
            scale = lax.rsqrt(jnp.mean(attended * attended, axis=-1, keepdims=True) + epsilon)
            unit = attended * scale
            held[here, cols] = (unit * gain).astype(BF16)
            pulled = cotangent[here, cols].astype(F32) * gain
            along = jnp.mean(pulled * unit, axis=-1, keepdims=True)
            grad_ref[here, cols] = (scale * (pulled - unit * along)).astype(BF16)
        rows_here = pl.ds(low, tile)
        copy = pltpu.make_async_copy(held.at[rows_here, :], normed_ref.at[rows_here, :], sems.at[low // tile])
        copy.start()
        outward.append(copy)
    place = lax.broadcasted_iota(jnp.int32, (rows, HEAD_DIM), 0)
    in_first = place < marks_ref[2 * blocks]
    for head in range(width // HEAD_DIM):
        cols = head_cols(head)
        q = queries[:, cols]
        kept = jnp.where(in_first, q, jnp.zeros_like(q))
        part_ref[cols, :] = dot(kept, grad_ref[:, cols], ROWS).astype(part_ref.dtype)
    for copy in outward:
        copy.wait()


def grad_q_kernel(blocks, marks_ref, span_ref, packed_ref, grad_ref, state_ref, ended_ref, grad_q_ref):
    ended_ref[...] = jnp.zeros_like(ended_ref)
    keys, values = unpacked(packed_ref, 0), unpacked(packed_ref, 1)
    rows, width = keys.shape
    for low in range(0, rows, TILE):
        high = low + TILE
        row = low + lax.broadcasted_iota(jnp.int32, (TILE, high), 0)
        column = lax.broadcasted_iota(jnp.int32, (TILE, high), 1)
        mask = (column <= row) & (row < span_ref[1:2, :high])
        place = low + lax.broadcasted_iota(jnp.int32, (TILE, HEAD_DIM), 0)
        carried = place < marks_ref[2 * blocks + 1]
        for head in range(width // HEAD_DIM):
            cols = head_cols(head)
            grad = grad_ref[low:high, cols]
            scores = dot(grad, values[:high, cols], FEATURES)
            grad_attn = jnp.where(mask, scores, 0.0).astype(BF16)
            inter = dot(grad, state_ref[cols, :], FEATURES)
            grad_q = dot(grad_attn, keys[:high, cols], PLAIN) + jnp.where(carried, inter, 0.0)
            grad_q_ref[low:high, cols] = grad_q.astype(BF16)


def grad_kv_kernel(span_ref, packed_ref, grad_ref, part_k_ref, part_v_ref):
    keys, values, queries = (unpacked(packed_ref, at) for at in range(3))
    rows, width = keys.shape
    for low in range(0, rows, TILE):
        high = low + TILE
        row = low + lax.broadcasted_iota(jnp.int32, (TILE, rows - low), 0)
        column = low + lax.broadcasted_iota(jnp.int32, (TILE, rows - low), 1)
        mask = (row <= column) & (row >= span_ref[0:1, low:])
        for head in range(width // HEAD_DIM):
            cols = head_cols(head)
            q, k, v = (field[:, cols] for field in (queries, keys, values))
            grad = grad_ref[:, cols]
            turned = dot(v[low:high], grad[low:], FEATURES)
            turned = jnp.where(mask, turned, 0.0).astype(BF16)
            part_k_ref[low:high, cols] = dot(turned, q[low:], PLAIN)
            turned = dot(k[low:high], q[low:], FEATURES)
            turned = jnp.where(mask, turned, 0.0).astype(BF16)
            part_v_ref[low:high, cols] = dot(turned, grad[low:], PLAIN)


def last_kernel(
    blocks, where_ref, marks_ref, packed_ref, part_k_ref, part_v_ref, far_ref, near_ref,
    grad_k_ref, grad_v_ref, held, sems,
):
    keys, values = unpacked(packed_ref, 0), unpacked(packed_ref, 1)
    back = entering(True, blocks, where_ref, marks_ref, far_ref, near_ref)
    rows, width = keys.shape
    outward = []
    for low in range(0, rows, TILE):
        here = slice(low, low + TILE)
        place = low + lax.broadcasted_iota(jnp.int32, (TILE, HEAD_DIM), 0)
        later = place >= marks_ref[2 * blocks + 3]
        for head in range(width // HEAD_DIM):
            cols = head_cols(head)
            inter = dot(values[here, cols], back[cols, :], FEATURES)
            held[0, here, cols] = (part_k_ref[here, cols] + jnp.where(later, inter, 0.0)).astype(BF16)
            inter = dot(keys[here, cols], back[cols, :], PLAIN)
            held[1, here, cols] = (part_v_ref[here, cols] + jnp.where(later, inter, 0.0)).astype(BF16)
        rows_here = pl.ds(low, TILE)
        for k, out_ref in enumerate((grad_k_ref, grad_v_ref)):
            copy = pltpu.make_async_copy(
                held.at[k, rows_here, :], out_ref.at[rows_here, :], sems.at[k, low // TILE]
            )
            copy.start()
            outward.append(copy)
    for copy in outward:
        copy.wait()


def unpack_kernel(parts_ref, ended_ref, out_ref):
    ended_ref[...] = jnp.zeros_like(ended_ref)
    groups, _, width = parts_ref.shape
    for group in range(groups):
        out_ref[:, group * width : (group + 1) * width] = parts_ref[group]


SMEM = pl.BlockSpec(memory_space=pltpu.SMEM)
VMEM = pl.BlockSpec(memory_space=pltpu.VMEM)
ANYWHERE = pl.BlockSpec(memory_space=pl.ANY)
ENDED = jax.ShapeDtypeStruct((8, HEAD_DIM), F32)


def call(
    kernel, name, outs, scalars, arrays, flops, scratch=(), after=(), in_specs=None, out_specs=None, limit=40, aliases=None
):
    moved = sum(a.size * a.dtype.itemsize for a in (*arrays, *outs))
    given = len(scalars) + len(arrays)

    def body(*refs):
        kernel(*refs[:given], *refs[given + len(after) :])

    return pl.pallas_call(
        body,
        name=name,
        out_shape=outs,
        in_specs=[SMEM] * len(scalars) + (in_specs or [VMEM] * len(arrays)) + [ANYWHERE] * len(after),
        out_specs=out_specs or [VMEM] * len(outs),
        scratch_shapes=list(scratch),
        input_output_aliases=aliases or {},
        compiler_params=pltpu.CompilerParams(vmem_limit_bytes=limit * 1024 * 1024),
        cost_estimate=pl.CostEstimate(flops=flops, bytes_accessed=moved, transcendentals=0),
    )(*scalars, *arrays, *after)


def across_head(parts):
    return lax.all_to_all(parts, "head", split_axis=0, concat_axis=0, tiled=True)


def to_heads(arrays, after):
    groups, count = lax.axis_size("head"), len(arrays)
    tokens, cols = arrays[0].shape
    ended, packed = call(
        pack_kernel,
        "pack",
        [ENDED, jax.ShapeDtypeStruct((groups, count * tokens, cols // groups), BF16)],
        [],
        arrays,
        0,
        [
            pltpu.VMEM((count, tokens, cols), BF16),
            pltpu.SemaphoreType.DMA((count,)),
            pltpu.SemaphoreType.DMA((count, groups)),
        ],
        after,
        [ANYWHERE] * count,
        [VMEM, ANYWHERE],
        60,
    )
    return ended, packed


def from_block(field, step):
    blocks = lax.axis_size("seq")
    return lax.ppermute(field, "seq", [(at, (at + step) % blocks) for at in range(blocks)])


def span(kernel, parts, where, marks, reverse, after=()):
    blocks = lax.axis_size("seq")
    return call(
        functools.partial(kernel, reverse, blocks),
        kernel.__name__.replace("kernel", "back" if reverse else "forward"),
        [jax.ShapeDtypeStruct(parts[0].shape, BF16)],
        [where, marks],
        parts,
        len(parts) * parts[0].size,
        after=after,
    )[0]


def span_of_three(part, where, marks, reverse, after=()):
    parts = [from_block(part, 1), part, from_block(part, -1)]
    if reverse:
        parts.reverse()
    return span(three_kernel, parts, where, marks, reverse, after)


def span_of_nine(three, where, marks, reverse, after=()):
    parts = [from_block(three, 3), three, from_block(three, -3)]
    if reverse:
        parts.reverse()
    return span(nine_kernel, parts, where, marks, reverse, after)


def two_spans(nine, reverse):
    sign = -1 if reverse else 1
    return [from_block(nine, sign * 14), from_block(nine, sign * 5)]


def on_device(queries, keys, values, cotangent, gain, lengths):
    groups, blocks = lax.axis_size("head"), lax.axis_size("seq")
    tokens, cols = queries.shape
    rows, width = tokens * groups, cols // groups
    square = rows * rows * width
    here = lax.axis_index("head").astype(jnp.int32)
    where = jnp.stack([lax.axis_index("seq").astype(jnp.int32), here])
    f32 = functools.partial(jax.ShapeDtypeStruct, dtype=F32)
    bf16 = functools.partial(jax.ShapeDtypeStruct, dtype=BF16)
    int32 = functools.partial(jax.ShapeDtypeStruct, dtype=jnp.int32)
    started, parts = call(
        parts_kernel,
        "parts",
        [ENDED, bf16((groups, width, HEAD_DIM))],
        [lengths, lax.axis_index("seq").astype(jnp.int32).reshape(1), here.reshape(1)],
        [keys, values],
        2 * tokens * cols * HEAD_DIM,
        [
            pltpu.VMEM((2, tokens, cols), BF16),
            pltpu.VMEM((groups, width, HEAD_DIM), BF16),
            pltpu.SemaphoreType.DMA((2,)),
            pltpu.SemaphoreType.DMA((groups,)),
        ],
        in_specs=[ANYWHERE] * 2,
        out_specs=[VMEM, ANYWHERE],
        limit=60,
    )
    (marks,) = call(
        functools.partial(meta_kernel, blocks, rows),
        "meta",
        [int32((2 * blocks + 4,))],
        [lengths, where],
        [],
        rows,
        after=[started],
        out_specs=[SMEM],
    )
    (docs,) = call(docs_kernel, "docs", [int32((2, rows))], [lengths, where, marks], [], rows)
    gathered = across_head(parts)
    ended, packed = to_heads([keys, values, queries, cotangent], [docs])
    (tail,) = call(
        tail_kernel,
        "tail",
        [bf16((width, HEAD_DIM))],
        [marks],
        [gathered],
        gathered.size,
        after=[ended],
    )
    packed = across_head(packed)
    three = span_of_three(tail, where, marks, False)
    before = two_spans(span_of_nine(three, where, marks, False), False)
    (inside,) = call(intra_kernel, "intra", [f32((rows, width))], [], [docs, packed], 2 * square)
    normed, grad, part, state = call(
        functools.partial(norm_kernel, blocks),
        "norm",
        [bf16((rows, width)), bf16((rows, width)), bf16((width, HEAD_DIM)), bf16((width, HEAD_DIM))],
        [where, marks],
        [packed, inside, gain.reshape(1, cols), *before],
        4 * rows * width * HEAD_DIM,
        [pltpu.VMEM((rows, width), BF16), pltpu.SemaphoreType.DMA((rows // HEAD_DIM,))],
        out_specs=[ANYWHERE, VMEM, VMEM, VMEM],
    )

    normed = across_head(normed.reshape(groups, tokens, width))
    ended, grad_q = call(
        functools.partial(grad_q_kernel, blocks),
        "grads_q",
        [ENDED, bf16((rows, width))],
        [marks],
        [docs, packed, grad, state],
        2 * square,
    )
    three = span_of_three(part, where, marks, True, [ended])
    nine = span_of_nine(three, where, marks, True)
    part_k, part_v = call(
        grad_kv_kernel,
        "grads_kv",
        [f32((rows, width)), f32((rows, width))],
        [],
        [docs, packed, grad],
        4 * square,
        after=[nine],
    )
    ended, normed = call(unpack_kernel, "unpack", [ENDED, bf16((tokens, cols))], [], [normed], 0)
    grad_k, grad_v = call(
        functools.partial(last_kernel, blocks),
        "last",
        [bf16((rows, width)), bf16((rows, width))],
        [where, marks],
        [packed, part_k, part_v, *two_spans(nine, True)],
        4 * rows * width * HEAD_DIM,
        [pltpu.VMEM((2, rows, width), BF16), pltpu.SemaphoreType.DMA((2, rows // TILE))],
        after=[ended],
        out_specs=[ANYWHERE] * 2,
    )
    return normed, grad_q, grad_k, grad_v


def solution(mesh):
    placed = P(("seq", "head"), None)
    return jax.shard_map(
        on_device,
        mesh=mesh,
        in_specs=(placed, placed, placed, placed, P(), P()),
        out_specs=(placed, P("seq", "head"), P("seq", "head"), P("seq", "head")),
        check_vma=False,
    )
```

```python
import functools

import jax
import jax.numpy as jnp
from jax import lax
from jax.experimental import pallas as pl
from jax.experimental.pallas import tpu as pltpu
from jax.sharding import PartitionSpec as P

HEAD_DIM = 128
TILE = 256


epsilon = 1e-05

F32 = jnp.float32
BF16 = jnp.bfloat16

ROWS = (((0,), (0,)), ((), ()))
FEATURES = (((1,), (1,)), ((), ()))
PLAIN = (((1,), (0,)), ((), ()))


def dot(a, b, dims):
    return lax.dot_general(a, b, dims, preferred_element_type=F32)


def unpacked(packed_ref, at):
    groups, stacked, width = packed_ref.shape
    tokens = stacked // 4
    return packed_ref[:, at * tokens : (at + 1) * tokens, :].reshape(groups * tokens, width)


def head_cols(head):
    return slice(head * HEAD_DIM, (head + 1) * HEAD_DIM)


def meta_kernel(blocks, rows, lengths_ref, where_ref, marks_ref):
    first = where_ref[0] * rows
    last = first + rows - 1

    def clear(i, carry):
        marks_ref[i] = 0
        return carry

    lax.fori_loop(0, 2 * blocks, clear, 0)
    marks_ref[2 * blocks - 1] = 1
    marks_ref[2 * blocks + 1] = 0
    marks_ref[2 * blocks + 3] = rows

    def step(i, begin):
        after = begin + lengths_ref[i]
        marks_ref[begin // rows] = 1
        marks_ref[blocks + jnp.maximum(begin - 1, 0) // rows] = 1

        @pl.when((begin <= first) & (first < after))
        def _():
            marks_ref[2 * blocks] = after - first
            marks_ref[2 * blocks + 1] = jnp.where(begin < first, after - first, 0)

        @pl.when((begin <= last) & (last < after))
        def _():
            marks_ref[2 * blocks + 2] = begin - first
            marks_ref[2 * blocks + 3] = jnp.where(after > last + 1, begin - first, rows)

        return after

    lax.fori_loop(0, lengths_ref.shape[0], step, jnp.int32(0))


def docs_kernel(lengths_ref, where_ref, marks_ref, span_ref):
    rows = span_ref.shape[1]
    first = where_ref[0] * rows
    place = first + lax.broadcasted_iota(jnp.int32, (1, rows), 1)

    def step(i, carry):
        begin, start, end = carry
        after = begin + lengths_ref[i]
        inside = (place >= begin) & (place < after)
        return (after, jnp.where(inside, begin, start), jnp.where(inside, after, end))

    zero = jnp.zeros((1, rows), jnp.int32)
    _, start, end = lax.fori_loop(0, lengths_ref.shape[0], step, (jnp.int32(0), zero, zero))
    span_ref[0:1, :] = start - first
    span_ref[1:2, :] = end - first


def pack_kernel(*refs):
    *arrays, ended_ref, out_ref, held, in_sems, out_sems = refs
    ended_ref[...] = jnp.zeros_like(ended_ref)
    groups, _, width = out_ref.shape
    tokens = arrays[0].shape[0]
    inward = [
        pltpu.make_async_copy(ref, held.at[k], in_sems.at[k]) for k, ref in enumerate(arrays)
    ]
    outward = [
        [
            pltpu.make_async_copy(
                held.at[k, :, pl.ds(at * width, width)],
                out_ref.at[at, pl.ds(k * tokens, tokens), :],
                out_sems.at[k, at],
            )
            for at in range(groups)
        ]
        for k in range(len(arrays))
    ]
    for copy in inward:
        copy.start()
    for copy, parts in zip(inward, outward):
        copy.wait()
        for part in parts:
            part.start()
    for parts in outward:
        for part in parts:
            part.wait()


def parts_kernel(
    lengths_ref, seq_ref, head_ref, keys_ref, values_ref, ended_ref, out_ref, held, sums, in_sems, out_sems
):
    inward = [
        pltpu.make_async_copy(ref, held.at[k], in_sems.at[k])
        for k, ref in enumerate((keys_ref, values_ref))
    ]
    for copy in inward:
        copy.start()
    ended_ref[...] = jnp.zeros_like(ended_ref)
    groups, width, _ = out_ref.shape
    tokens, cols = keys_ref.shape
    last = (seq_ref[0] + 1) * (tokens * groups) - 1
    begin, bound = jnp.int32(0), jnp.int32(0)
    for i in range(lengths_ref.shape[0]):
        bound = jnp.where(begin <= last, begin, bound)
        begin = begin + lengths_ref[i]
    mine = last + 1 - (groups - head_ref[0]) * tokens
    place = mine + lax.broadcasted_iota(jnp.int32, (tokens, HEAD_DIM), 0)
    for copy in inward:
        copy.wait()
    outward = []
    for group in range(groups):
        for head in range(width // HEAD_DIM):
            at = slice(group * width + head * HEAD_DIM, group * width + (head + 1) * HEAD_DIM)
            keys = held[0, :, at]
            keys = jnp.where(place >= bound, keys, jnp.zeros_like(keys))
            part = dot(keys, held[1, :, at], ROWS)
            sums[group, head_cols(head), :] = part.astype(sums.dtype)
        copy = pltpu.make_async_copy(sums.at[group], out_ref.at[group], out_sems.at[group])
        copy.start()
        outward.append(copy)
    for copy in outward:
        copy.wait()


def tail_kernel(marks_ref, parts_ref, tail_ref):
    total = parts_ref[0].astype(F32)
    for k in range(1, parts_ref.shape[0]):
        total = total + parts_ref[k].astype(F32)
    tail_ref[...] = total.astype(tail_ref.dtype)


def block_mark(marks_ref, blocks, at, reverse):
    return marks_ref[lax.rem(at + blocks, blocks) + (blocks if reverse else 0)]


def chained(reverse, blocks, where_ref, marks_ref, refs, covers):
    mine, sign = where_ref[0], -1 if reverse else 1
    total = refs[0][...].astype(F32)
    for ref, (low, high) in zip(refs[1:], covers[1:]):
        mark = jnp.int32(0)
        for at in range(low, high + 1):
            mark = jnp.maximum(mark, block_mark(marks_ref, blocks, mine + sign * at, reverse))
        total = jnp.where(mark > 0, 0.0, total) + ref[...].astype(F32)
    return total.astype(BF16)


def three_kernel(reverse, blocks, where_ref, marks_ref, *refs):
    *parts, span_ref = refs
    covers = ((-1, -1), (0, 0), (1, 1))
    span_ref[...] = chained(reverse, blocks, where_ref, marks_ref, parts, covers)


def nine_kernel(reverse, blocks, where_ref, marks_ref, *refs):
    *parts, span_ref = refs
    covers = ((-4, -2), (-1, 1), (2, 4))
    span_ref[...] = chained(reverse, blocks, where_ref, marks_ref, parts, covers)


def entering(reverse, blocks, where_ref, marks_ref, *refs):
    return chained(reverse, blocks, where_ref, marks_ref, refs, ((-18, -10), (-9, -1)))


def intra_kernel(span_ref, packed_ref, intra_ref):
    keys, values, queries = (unpacked(packed_ref, at) for at in range(3))
    rows, width = keys.shape
    for low in range(0, rows, TILE):
        high = low + TILE
        row = low + lax.broadcasted_iota(jnp.int32, (TILE, high), 0)
        column = lax.broadcasted_iota(jnp.int32, (TILE, high), 1)
        mask = (column <= row) & (row < span_ref[1:2, :high])
        for head in range(width // HEAD_DIM):
            cols = head_cols(head)
            scores = dot(queries[low:high, cols], keys[:high, cols], FEATURES)
            attn = jnp.where(mask, scores, 0.0).astype(BF16)
            intra_ref[low:high, cols] = dot(attn, values[:high, cols], PLAIN)


def norm_kernel(blocks, where_ref, marks_ref, packed_ref, intra_ref, gain_ref, *refs):
    far_ref, near_ref, normed_ref, grad_ref, part_ref, state_ref = refs
    queries, cotangent = unpacked(packed_ref, 2), unpacked(packed_ref, 3)
    state = entering(False, blocks, where_ref, marks_ref, far_ref, near_ref)
    state_ref[...] = state
    rows, width = intra_ref.shape
    tile = HEAD_DIM
    for head in range(width // HEAD_DIM):
        cols = head_cols(head)
        at = pl.multiple_of(where_ref[1] * width + head * HEAD_DIM, HEAD_DIM)
        gain = gain_ref[:, pl.ds(at, HEAD_DIM)]
        for low in range(0, rows, tile):
            here = slice(low, low + tile)
            place = low + lax.broadcasted_iota(jnp.int32, (tile, HEAD_DIM), 0)
            inter = dot(queries[here, cols], state[cols, :], PLAIN)
            inter = jnp.where(place < marks_ref[2 * blocks + 1], inter, 0.0)
            attended = intra_ref[here, cols] + inter
            scale = lax.rsqrt(jnp.mean(attended * attended, axis=-1, keepdims=True) + epsilon)
            unit = attended * scale
            normed_ref[here, cols] = (unit * gain).astype(BF16)
            pulled = cotangent[here, cols].astype(F32) * gain
            along = jnp.mean(pulled * unit, axis=-1, keepdims=True)
            grad_ref[here, cols] = (scale * (pulled - unit * along)).astype(BF16)
    place = lax.broadcasted_iota(jnp.int32, (rows, HEAD_DIM), 0)
    in_first = place < marks_ref[2 * blocks]
    for head in range(width // HEAD_DIM):
        cols = head_cols(head)
        q = queries[:, cols]
        kept = jnp.where(in_first, q, jnp.zeros_like(q))
        part_ref[cols, :] = dot(kept, grad_ref[:, cols], ROWS).astype(part_ref.dtype)


def grad_q_kernel(blocks, marks_ref, span_ref, packed_ref, grad_ref, state_ref, ended_ref, grad_q_ref):
    ended_ref[...] = jnp.zeros_like(ended_ref)
    keys, values = unpacked(packed_ref, 0), unpacked(packed_ref, 1)
    rows, width = keys.shape
    for low in range(0, rows, TILE):
        high = low + TILE
        row = low + lax.broadcasted_iota(jnp.int32, (TILE, high), 0)
        column = lax.broadcasted_iota(jnp.int32, (TILE, high), 1)
        mask = (column <= row) & (row < span_ref[1:2, :high])
        place = low + lax.broadcasted_iota(jnp.int32, (TILE, HEAD_DIM), 0)
        carried = place < marks_ref[2 * blocks + 1]
        for head in range(width // HEAD_DIM):
            cols = head_cols(head)
            grad = grad_ref[low:high, cols]
            scores = dot(grad, values[:high, cols], FEATURES)
            grad_attn = jnp.where(mask, scores, 0.0).astype(BF16)
            inter = dot(grad, state_ref[cols, :], FEATURES)
            grad_q = dot(grad_attn, keys[:high, cols], PLAIN) + jnp.where(carried, inter, 0.0)
            grad_q_ref[low:high, cols] = grad_q.astype(BF16)


def grad_kv_kernel(span_ref, packed_ref, grad_ref, part_k_ref, part_v_ref):
    keys, values, queries = (unpacked(packed_ref, at) for at in range(3))
    rows, width = keys.shape
    for low in range(0, rows, TILE):
        high = low + TILE
        row = low + lax.broadcasted_iota(jnp.int32, (TILE, rows - low), 0)
        column = low + lax.broadcasted_iota(jnp.int32, (TILE, rows - low), 1)
        mask = (row <= column) & (row >= span_ref[0:1, low:])
        for head in range(width // HEAD_DIM):
            cols = head_cols(head)
            q, k, v = (field[:, cols] for field in (queries, keys, values))
            grad = grad_ref[:, cols]
            turned = dot(v[low:high], grad[low:], FEATURES)
            turned = jnp.where(mask, turned, 0.0).astype(BF16)
            part_k_ref[low:high, cols] = dot(turned, q[low:], PLAIN)
            turned = dot(k[low:high], q[low:], FEATURES)
            turned = jnp.where(mask, turned, 0.0).astype(BF16)
            part_v_ref[low:high, cols] = dot(turned, grad[low:], PLAIN)


def last_kernel(
    blocks, where_ref, marks_ref, packed_ref, part_k_ref, part_v_ref, far_ref, near_ref, grad_k_ref, grad_v_ref
):
    keys, values = unpacked(packed_ref, 0), unpacked(packed_ref, 1)
    back = entering(True, blocks, where_ref, marks_ref, far_ref, near_ref)
    rows, width = keys.shape
    place = lax.broadcasted_iota(jnp.int32, (rows, HEAD_DIM), 0)
    later = place >= marks_ref[2 * blocks + 3]
    for head in range(width // HEAD_DIM):
        cols = head_cols(head)
        inter = dot(values[:, cols], back[cols, :], FEATURES)
        grad_k_ref[:, cols] = (part_k_ref[:, cols] + jnp.where(later, inter, 0.0)).astype(BF16)
        inter = dot(keys[:, cols], back[cols, :], PLAIN)
        grad_v_ref[:, cols] = (part_v_ref[:, cols] + jnp.where(later, inter, 0.0)).astype(BF16)


SMEM = pl.BlockSpec(memory_space=pltpu.SMEM)
VMEM = pl.BlockSpec(memory_space=pltpu.VMEM)
ANYWHERE = pl.BlockSpec(memory_space=pl.ANY)
ENDED = jax.ShapeDtypeStruct((8, HEAD_DIM), F32)


def call(
    kernel, name, outs, scalars, arrays, flops, scratch=(), after=(), in_specs=None, out_specs=None, limit=40, aliases=None
):
    moved = sum(a.size * a.dtype.itemsize for a in (*arrays, *outs))
    given = len(scalars) + len(arrays)

    def body(*refs):
        kernel(*refs[:given], *refs[given + len(after) :])

    return pl.pallas_call(
        body,
        name=name,
        out_shape=outs,
        in_specs=[SMEM] * len(scalars) + (in_specs or [VMEM] * len(arrays)) + [ANYWHERE] * len(after),
        out_specs=out_specs or [VMEM] * len(outs),
        scratch_shapes=list(scratch),
        input_output_aliases=aliases or {},
        compiler_params=pltpu.CompilerParams(vmem_limit_bytes=limit * 1024 * 1024),
        cost_estimate=pl.CostEstimate(flops=flops, bytes_accessed=moved, transcendentals=0),
    )(*scalars, *arrays, *after)


def across_head(parts):
    return lax.all_to_all(parts, "head", split_axis=0, concat_axis=0, tiled=True)


def to_heads(arrays, after):
    groups, count = lax.axis_size("head"), len(arrays)
    tokens, cols = arrays[0].shape
    ended, packed = call(
        pack_kernel,
        "pack",
        [ENDED, jax.ShapeDtypeStruct((groups, count * tokens, cols // groups), BF16)],
        [],
        arrays,
        0,
        [
            pltpu.VMEM((count, tokens, cols), BF16),
            pltpu.SemaphoreType.DMA((count,)),
            pltpu.SemaphoreType.DMA((count, groups)),
        ],
        after,
        [ANYWHERE] * count,
        [VMEM, ANYWHERE],
        60,
    )
    return ended, packed


def from_block(field, step):
    blocks = lax.axis_size("seq")
    return lax.ppermute(field, "seq", [(at, (at + step) % blocks) for at in range(blocks)])


def span(kernel, parts, where, marks, reverse, after=()):
    blocks = lax.axis_size("seq")
    return call(
        functools.partial(kernel, reverse, blocks),
        kernel.__name__.replace("kernel", "back" if reverse else "forward"),
        [jax.ShapeDtypeStruct(parts[0].shape, BF16)],
        [where, marks],
        parts,
        len(parts) * parts[0].size,
        after=after,
    )[0]


def span_of_three(part, where, marks, reverse, after=()):
    parts = [from_block(part, 1), part, from_block(part, -1)]
    if reverse:
        parts.reverse()
    return span(three_kernel, parts, where, marks, reverse, after)


def span_of_nine(three, where, marks, reverse, after=()):
    parts = [from_block(three, 3), three, from_block(three, -3)]
    if reverse:
        parts.reverse()
    return span(nine_kernel, parts, where, marks, reverse, after)


def two_spans(nine, reverse):
    sign = -1 if reverse else 1
    return [from_block(nine, sign * 14), from_block(nine, sign * 5)]


def on_device(queries, keys, values, cotangent, gain, lengths):
    groups, blocks = lax.axis_size("head"), lax.axis_size("seq")
    tokens, cols = queries.shape
    rows, width = tokens * groups, cols // groups
    square = rows * rows * width
    here = lax.axis_index("head").astype(jnp.int32)
    where = jnp.stack([lax.axis_index("seq").astype(jnp.int32), here])
    f32 = functools.partial(jax.ShapeDtypeStruct, dtype=F32)
    bf16 = functools.partial(jax.ShapeDtypeStruct, dtype=BF16)
    int32 = functools.partial(jax.ShapeDtypeStruct, dtype=jnp.int32)
    started, parts = call(
        parts_kernel,
        "parts",
        [ENDED, bf16((groups, width, HEAD_DIM))],
        [lengths, lax.axis_index("seq").astype(jnp.int32).reshape(1), here.reshape(1)],
        [keys, values],
        2 * tokens * cols * HEAD_DIM,
        [
            pltpu.VMEM((2, tokens, cols), BF16),
            pltpu.VMEM((groups, width, HEAD_DIM), BF16),
            pltpu.SemaphoreType.DMA((2,)),
            pltpu.SemaphoreType.DMA((groups,)),
        ],
        in_specs=[ANYWHERE] * 2,
        out_specs=[VMEM, ANYWHERE],
        limit=60,
    )
    (marks,) = call(
        functools.partial(meta_kernel, blocks, rows),
        "meta",
        [int32((2 * blocks + 4,))],
        [lengths, where],
        [],
        rows,
        after=[started],
        out_specs=[SMEM],
    )
    (docs,) = call(docs_kernel, "docs", [int32((2, rows))], [lengths, where, marks], [], rows)
    gathered = across_head(parts)
    ended, packed = to_heads([keys, values, queries, cotangent], [docs])
    (tail,) = call(
        tail_kernel,
        "tail",
        [bf16((width, HEAD_DIM))],
        [marks],
        [gathered],
        gathered.size,
        after=[ended],
    )
    packed = across_head(packed)
    three = span_of_three(tail, where, marks, False)
    before = two_spans(span_of_nine(three, where, marks, False), False)
    (inside,) = call(intra_kernel, "intra", [f32((rows, width))], [], [docs, packed], 2 * square)
    normed, grad, part, state = call(
        functools.partial(norm_kernel, blocks),
        "norm",
        [bf16((rows, width)), bf16((rows, width)), bf16((width, HEAD_DIM)), bf16((width, HEAD_DIM))],
        [where, marks],
        [packed, inside, gain.reshape(1, cols), *before],
        4 * rows * width * HEAD_DIM,
    )

    normed = across_head(normed.reshape(groups, tokens, width))
    ended, grad_q = call(
        functools.partial(grad_q_kernel, blocks),
        "grads_q",
        [ENDED, bf16((rows, width))],
        [marks],
        [docs, packed, grad, state],
        2 * square,
    )
    three = span_of_three(part, where, marks, True, [ended])
    nine = span_of_nine(three, where, marks, True)
    part_k, part_v = call(
        grad_kv_kernel,
        "grads_kv",
        [f32((rows, width)), f32((rows, width))],
        [],
        [docs, packed, grad],
        4 * square,
        after=[nine],
    )
    grad_k, grad_v = call(
        functools.partial(last_kernel, blocks),
        "last",
        [bf16((rows, width)), bf16((rows, width))],
        [where, marks],
        [packed, part_k, part_v, *two_spans(nine, True)],
        4 * rows * width * HEAD_DIM,
    )
    return normed.transpose(1, 0, 2).reshape(tokens, cols), grad_q, grad_k, grad_v


def solution(mesh):
    placed = P(("seq", "head"), None)
    return jax.shard_map(
        on_device,
        mesh=mesh,
        in_specs=(placed, placed, placed, placed, P(), P()),
        out_specs=(placed, P("seq", "head"), P("seq", "head"), P("seq", "head")),
        check_vma=False,
    )
```

```python
import functools

import jax
import jax.numpy as jnp
from jax import lax
from jax.experimental import pallas as pl
from jax.experimental.pallas import tpu as pltpu
from jax.sharding import PartitionSpec as P

HEAD_DIM = 128
TILE = 256


epsilon = 1e-05

F32 = jnp.float32
BF16 = jnp.bfloat16

ROWS = (((0,), (0,)), ((), ()))
FEATURES = (((1,), (1,)), ((), ()))
PLAIN = (((1,), (0,)), ((), ()))


def dot(a, b, dims):
    return lax.dot_general(a, b, dims, preferred_element_type=F32)


def unpacked(packed_ref, at):
    groups, stacked, width = packed_ref.shape
    tokens = stacked // 4
    return packed_ref[:, at * tokens : (at + 1) * tokens, :].reshape(groups * tokens, width)


def head_cols(head):
    return slice(head * HEAD_DIM, (head + 1) * HEAD_DIM)


def meta_kernel(blocks, rows, lengths_ref, where_ref, marks_ref):
    first = where_ref[0] * rows
    last = first + rows - 1

    def clear(i, carry):
        marks_ref[i] = 0
        return carry

    lax.fori_loop(0, 2 * blocks, clear, 0)
    marks_ref[2 * blocks - 1] = 1
    marks_ref[2 * blocks + 1] = 0
    marks_ref[2 * blocks + 3] = rows

    def step(i, begin):
        after = begin + lengths_ref[i]
        marks_ref[begin // rows] = 1
        marks_ref[blocks + jnp.maximum(begin - 1, 0) // rows] = 1

        @pl.when((begin <= first) & (first < after))
        def _():
            marks_ref[2 * blocks] = after - first
            marks_ref[2 * blocks + 1] = jnp.where(begin < first, after - first, 0)

        @pl.when((begin <= last) & (last < after))
        def _():
            marks_ref[2 * blocks + 2] = begin - first
            marks_ref[2 * blocks + 3] = jnp.where(after > last + 1, begin - first, rows)

        return after

    lax.fori_loop(0, lengths_ref.shape[0], step, jnp.int32(0))


def docs_kernel(lengths_ref, where_ref, marks_ref, span_ref):
    rows = span_ref.shape[1]
    first = where_ref[0] * rows
    place = first + lax.broadcasted_iota(jnp.int32, (1, rows), 1)

    def step(i, carry):
        begin, start, end = carry
        after = begin + lengths_ref[i]
        inside = (place >= begin) & (place < after)
        return (after, jnp.where(inside, begin, start), jnp.where(inside, after, end))

    zero = jnp.zeros((1, rows), jnp.int32)
    _, start, end = lax.fori_loop(0, lengths_ref.shape[0], step, (jnp.int32(0), zero, zero))
    span_ref[0:1, :] = start - first
    span_ref[1:2, :] = end - first


def pack_kernel(*refs):
    *arrays, ended_ref, out_ref, held, in_sems, out_sems = refs
    ended_ref[...] = jnp.zeros_like(ended_ref)
    groups, _, width = out_ref.shape
    tokens = arrays[0].shape[0]
    inward = [
        pltpu.make_async_copy(ref, held.at[k], in_sems.at[k]) for k, ref in enumerate(arrays)
    ]
    outward = [
        [
            pltpu.make_async_copy(
                held.at[k, :, pl.ds(at * width, width)],
                out_ref.at[at, pl.ds(k * tokens, tokens), :],
                out_sems.at[k, at],
            )
            for at in range(groups)
        ]
        for k in range(len(arrays))
    ]
    for copy in inward:
        copy.start()
    for copy, parts in zip(inward, outward):
        copy.wait()
        for part in parts:
            part.start()
    for parts in outward:
        for part in parts:
            part.wait()


def parts_kernel(lengths_ref, seq_ref, head_ref, keys_ref, values_ref, ended_ref, out_ref, held, sems):
    copies = [
        pltpu.make_async_copy(ref, held.at[k], sems.at[k])
        for k, ref in enumerate((keys_ref, values_ref))
    ]
    for copy in copies:
        copy.start()
    ended_ref[...] = jnp.zeros_like(ended_ref)
    groups, width, _ = out_ref.shape
    tokens, cols = keys_ref.shape
    last = (seq_ref[0] + 1) * (tokens * groups) - 1
    begin, bound = jnp.int32(0), jnp.int32(0)
    for i in range(lengths_ref.shape[0]):
        bound = jnp.where(begin <= last, begin, bound)
        begin = begin + lengths_ref[i]
    mine = last + 1 - (groups - head_ref[0]) * tokens
    for copy in copies:
        copy.wait()
    place = mine + lax.broadcasted_iota(jnp.int32, (tokens, cols), 0)
    keys = held[0]
    keys = jnp.where(place >= bound, keys, jnp.zeros_like(keys))
    for head in range(cols // HEAD_DIM):
        part = dot(keys[:, head_cols(head)], held[1, :, head_cols(head)], ROWS)
        group, at = divmod(head * HEAD_DIM, width)
        out_ref[group, at : at + HEAD_DIM, :] = part.astype(out_ref.dtype)


def tail_kernel(marks_ref, parts_ref, tail_ref):
    total = parts_ref[0].astype(F32)
    for k in range(1, parts_ref.shape[0]):
        total = total + parts_ref[k].astype(F32)
    tail_ref[...] = total.astype(tail_ref.dtype)


def block_mark(marks_ref, blocks, at, reverse):
    return marks_ref[lax.rem(at + blocks, blocks) + (blocks if reverse else 0)]


def chained(reverse, blocks, where_ref, marks_ref, refs, covers):
    mine, sign = where_ref[0], -1 if reverse else 1
    total = refs[0][...].astype(F32)
    for ref, (low, high) in zip(refs[1:], covers[1:]):
        mark = jnp.int32(0)
        for at in range(low, high + 1):
            mark = jnp.maximum(mark, block_mark(marks_ref, blocks, mine + sign * at, reverse))
        total = jnp.where(mark > 0, 0.0, total) + ref[...].astype(F32)
    return total.astype(BF16)


def three_kernel(reverse, blocks, where_ref, marks_ref, *refs):
    *parts, span_ref = refs
    covers = ((-1, -1), (0, 0), (1, 1))
    span_ref[...] = chained(reverse, blocks, where_ref, marks_ref, parts, covers)


def nine_kernel(reverse, blocks, where_ref, marks_ref, *refs):
    *parts, span_ref = refs
    covers = ((-4, -2), (-1, 1), (2, 4))
    span_ref[...] = chained(reverse, blocks, where_ref, marks_ref, parts, covers)


def entering(reverse, blocks, where_ref, marks_ref, *refs):
    return chained(reverse, blocks, where_ref, marks_ref, refs, ((-18, -10), (-9, -1)))


def intra_kernel(span_ref, packed_ref, intra_ref):
    keys, values, queries = (unpacked(packed_ref, at) for at in range(3))
    rows, width = keys.shape
    for low in range(0, rows, TILE):
        high = low + TILE
        row = low + lax.broadcasted_iota(jnp.int32, (TILE, high), 0)
        column = lax.broadcasted_iota(jnp.int32, (TILE, high), 1)
        mask = (column <= row) & (row < span_ref[1:2, :high])
        for head in range(width // HEAD_DIM):
            cols = head_cols(head)
            scores = dot(queries[low:high, cols], keys[:high, cols], FEATURES)
            attn = jnp.where(mask, scores, 0.0).astype(BF16)
            intra_ref[low:high, cols] = dot(attn, values[:high, cols], PLAIN)


def norm_kernel(blocks, where_ref, marks_ref, packed_ref, intra_ref, gain_ref, *refs):
    far_ref, near_ref, normed_ref, grad_ref, part_ref, state_ref = refs
    queries, cotangent = unpacked(packed_ref, 2), unpacked(packed_ref, 3)
    state = entering(False, blocks, where_ref, marks_ref, far_ref, near_ref)
    state_ref[...] = state
    rows, width = intra_ref.shape
    tile = HEAD_DIM
    for head in range(width // HEAD_DIM):
        cols = head_cols(head)
        at = pl.multiple_of(where_ref[1] * width + head * HEAD_DIM, HEAD_DIM)
        gain = gain_ref[:, pl.ds(at, HEAD_DIM)]
        for low in range(0, rows, tile):
            here = slice(low, low + tile)
            place = low + lax.broadcasted_iota(jnp.int32, (tile, HEAD_DIM), 0)
            inter = dot(queries[here, cols], state[cols, :], PLAIN)
            inter = jnp.where(place < marks_ref[2 * blocks + 1], inter, 0.0)
            attended = intra_ref[here, cols] + inter
            scale = lax.rsqrt(jnp.mean(attended * attended, axis=-1, keepdims=True) + epsilon)
            unit = attended * scale
            normed_ref[here, cols] = (unit * gain).astype(BF16)
            pulled = cotangent[here, cols].astype(F32) * gain
            along = jnp.mean(pulled * unit, axis=-1, keepdims=True)
            grad_ref[here, cols] = (scale * (pulled - unit * along)).astype(BF16)
    place = lax.broadcasted_iota(jnp.int32, (rows, HEAD_DIM), 0)
    in_first = place < marks_ref[2 * blocks]
    for head in range(width // HEAD_DIM):
        cols = head_cols(head)
        q = queries[:, cols]
        kept = jnp.where(in_first, q, jnp.zeros_like(q))
        part_ref[cols, :] = dot(kept, grad_ref[:, cols], ROWS).astype(part_ref.dtype)


def grad_q_kernel(blocks, marks_ref, span_ref, packed_ref, grad_ref, state_ref, ended_ref, grad_q_ref):
    ended_ref[...] = jnp.zeros_like(ended_ref)
    keys, values = unpacked(packed_ref, 0), unpacked(packed_ref, 1)
    rows, width = keys.shape
    for low in range(0, rows, TILE):
        high = low + TILE
        row = low + lax.broadcasted_iota(jnp.int32, (TILE, high), 0)
        column = lax.broadcasted_iota(jnp.int32, (TILE, high), 1)
        mask = (column <= row) & (row < span_ref[1:2, :high])
        place = low + lax.broadcasted_iota(jnp.int32, (TILE, HEAD_DIM), 0)
        carried = place < marks_ref[2 * blocks + 1]
        for head in range(width // HEAD_DIM):
            cols = head_cols(head)
            grad = grad_ref[low:high, cols]
            scores = dot(grad, values[:high, cols], FEATURES)
            grad_attn = jnp.where(mask, scores, 0.0).astype(BF16)
            inter = dot(grad, state_ref[cols, :], FEATURES)
            grad_q = dot(grad_attn, keys[:high, cols], PLAIN) + jnp.where(carried, inter, 0.0)
            grad_q_ref[low:high, cols] = grad_q.astype(BF16)


def turned_kernel(docs_ref, left_ref, right_ref, rows_ref, ended_ref, part_ref):
    ended_ref[...] = jnp.zeros_like(ended_ref)
    left, right, summed = (
        unpacked(*field) if isinstance(field, tuple) else field for field in (left_ref, right_ref, rows_ref)
    )
    rows, width = part_ref.shape
    for low in range(0, rows, TILE):
        high = low + TILE
        row = low + lax.broadcasted_iota(jnp.int32, (TILE, rows - low), 0)
        column = low + lax.broadcasted_iota(jnp.int32, (TILE, rows - low), 1)
        mask = (row <= column) & (row >= docs_ref[0:1, low:])
        for head in range(width // HEAD_DIM):
            cols = head_cols(head)
            turned = dot(left[low:high, cols], right[low:, cols], FEATURES)
            turned = jnp.where(mask, turned, 0.0).astype(BF16)
            part_ref[low:high, cols] = dot(turned, summed[low:, cols], PLAIN)


def grad_k_kernel(docs_ref, packed_ref, grad_ref, ended_ref, part_ref):
    turned_kernel(docs_ref, (packed_ref, 1), grad_ref, (packed_ref, 2), ended_ref, part_ref)


def grad_v_kernel(docs_ref, packed_ref, grad_ref, ended_ref, part_ref):
    turned_kernel(docs_ref, (packed_ref, 0), (packed_ref, 2), grad_ref, ended_ref, part_ref)


def last_kernel(
    blocks, where_ref, marks_ref, packed_ref, part_k_ref, part_v_ref, far_ref, near_ref, grad_k_ref, grad_v_ref
):
    keys, values = unpacked(packed_ref, 0), unpacked(packed_ref, 1)
    back = entering(True, blocks, where_ref, marks_ref, far_ref, near_ref)
    rows, width = keys.shape
    place = lax.broadcasted_iota(jnp.int32, (rows, HEAD_DIM), 0)
    later = place >= marks_ref[2 * blocks + 3]
    for head in range(width // HEAD_DIM):
        cols = head_cols(head)
        inter = dot(values[:, cols], back[cols, :], FEATURES)
        grad_k_ref[:, cols] = (part_k_ref[:, cols] + jnp.where(later, inter, 0.0)).astype(BF16)
        inter = dot(keys[:, cols], back[cols, :], PLAIN)
        grad_v_ref[:, cols] = (part_v_ref[:, cols] + jnp.where(later, inter, 0.0)).astype(BF16)


SMEM = pl.BlockSpec(memory_space=pltpu.SMEM)
VMEM = pl.BlockSpec(memory_space=pltpu.VMEM)
ANYWHERE = pl.BlockSpec(memory_space=pl.ANY)
ENDED = jax.ShapeDtypeStruct((8, HEAD_DIM), F32)


def call(
    kernel, name, outs, scalars, arrays, flops, scratch=(), after=(), in_specs=None, out_specs=None, limit=40, aliases=None
):
    moved = sum(a.size * a.dtype.itemsize for a in (*arrays, *outs))
    given = len(scalars) + len(arrays)

    def body(*refs):
        kernel(*refs[:given], *refs[given + len(after) :])

    return pl.pallas_call(
        body,
        name=name,
        out_shape=outs,
        in_specs=[SMEM] * len(scalars) + (in_specs or [VMEM] * len(arrays)) + [ANYWHERE] * len(after),
        out_specs=out_specs or [VMEM] * len(outs),
        scratch_shapes=list(scratch),
        input_output_aliases=aliases or {},
        compiler_params=pltpu.CompilerParams(vmem_limit_bytes=limit * 1024 * 1024),
        cost_estimate=pl.CostEstimate(flops=flops, bytes_accessed=moved, transcendentals=0),
    )(*scalars, *arrays, *after)


def across_head(parts):
    return lax.all_to_all(parts, "head", split_axis=0, concat_axis=0, tiled=True)


def to_heads(arrays, after):
    groups, count = lax.axis_size("head"), len(arrays)
    tokens, cols = arrays[0].shape
    ended, packed = call(
        pack_kernel,
        "pack",
        [ENDED, jax.ShapeDtypeStruct((groups, count * tokens, cols // groups), BF16)],
        [],
        arrays,
        0,
        [
            pltpu.VMEM((count, tokens, cols), BF16),
            pltpu.SemaphoreType.DMA((count,)),
            pltpu.SemaphoreType.DMA((count, groups)),
        ],
        after,
        [ANYWHERE] * count,
        [VMEM, ANYWHERE],
        60,
    )
    return ended, packed


def from_block(field, step, reach, reverse):
    blocks = lax.axis_size("seq")
    pairs = []
    for at in range(blocks):
        to = at + step
        if to < blocks or to - blocks - step + reach >= 0:
            pairs.append((at, to % blocks))
    if reverse:
        pairs = [(blocks - 1 - at, blocks - 1 - to) for at, to in pairs]
    return lax.ppermute(field, "seq", pairs)


def span(kernel, parts, where, marks, reverse, after=()):
    blocks = lax.axis_size("seq")
    return call(
        functools.partial(kernel, reverse, blocks),
        kernel.__name__.replace("kernel", "back" if reverse else "forward"),
        [jax.ShapeDtypeStruct(parts[0].shape, BF16)],
        [where, marks],
        parts,
        len(parts) * parts[0].size,
        after=after,
    )[0]


def span_of_three(part, where, marks, reverse, after=()):
    parts = [from_block(part, 1, 0, reverse), part, from_block(part, -1, 0, reverse)]
    return span(three_kernel, parts, where, marks, reverse, after)


def span_of_nine(three, where, marks, reverse, after=()):
    parts = [from_block(three, 3, 1, reverse), three, from_block(three, -3, 1, reverse)]
    return span(nine_kernel, parts, where, marks, reverse, after)


def two_spans(nine, reverse):
    return [from_block(nine, 14, 4, reverse), from_block(nine, 5, 4, reverse)]


def on_device(queries, keys, values, cotangent, gain, lengths):
    groups, blocks = lax.axis_size("head"), lax.axis_size("seq")
    tokens, cols = queries.shape
    rows, width = tokens * groups, cols // groups
    square = rows * rows * width
    here = lax.axis_index("head").astype(jnp.int32)
    where = jnp.stack([lax.axis_index("seq").astype(jnp.int32), here])
    f32 = functools.partial(jax.ShapeDtypeStruct, dtype=F32)
    bf16 = functools.partial(jax.ShapeDtypeStruct, dtype=BF16)
    int32 = functools.partial(jax.ShapeDtypeStruct, dtype=jnp.int32)
    started, parts = call(
        parts_kernel,
        "parts",
        [ENDED, bf16((groups, width, HEAD_DIM))],
        [lengths, lax.axis_index("seq").astype(jnp.int32).reshape(1), here.reshape(1)],
        [keys, values],
        2 * tokens * cols * HEAD_DIM,
        [
            pltpu.VMEM((2, tokens, cols), BF16),
            pltpu.SemaphoreType.DMA((2,)),
        ],
        in_specs=[ANYWHERE] * 2,
        limit=60,
    )
    (marks,) = call(
        functools.partial(meta_kernel, blocks, rows),
        "meta",
        [int32((2 * blocks + 4,))],
        [lengths, where],
        [],
        rows,
        after=[started],
        out_specs=[SMEM],
    )
    (docs,) = call(docs_kernel, "docs", [int32((2, rows))], [lengths, where, marks], [], rows)
    gathered = across_head(parts)
    ended, packed = to_heads([keys, values, queries, cotangent], [docs])
    (tail,) = call(
        tail_kernel,
        "tail",
        [bf16((width, HEAD_DIM))],
        [marks],
        [gathered],
        gathered.size,
        after=[ended],
    )
    packed = across_head(packed)
    three = span_of_three(tail, where, marks, False)
    before = two_spans(span_of_nine(three, where, marks, False), False)
    (inside,) = call(intra_kernel, "intra", [f32((rows, width))], [], [docs, packed], 2 * square)
    normed, grad, part, state = call(
        functools.partial(norm_kernel, blocks),
        "norm",
        [bf16((rows, width)), bf16((rows, width)), bf16((width, HEAD_DIM)), bf16((width, HEAD_DIM))],
        [where, marks],
        [packed, inside, gain.reshape(1, cols), *before],
        4 * rows * width * HEAD_DIM,
    )

    normed = across_head(normed.reshape(groups, tokens, width))
    ended, grad_q = call(
        functools.partial(grad_q_kernel, blocks),
        "grads_q",
        [ENDED, bf16((rows, width))],
        [marks],
        [docs, packed, grad, state],
        2 * square,
    )
    three = span_of_three(part, where, marks, True, [ended])

    def turned(kernel, name, after):
        outs = [ENDED, f32((rows, width))]
        return call(kernel, name, outs, [], [docs, packed, grad], 2 * square, after=[after])

    ended, part_k = turned(grad_k_kernel, "grads_k", three)
    nine = span_of_nine(three, where, marks, True, [ended])
    _, part_v = turned(grad_v_kernel, "grads_v", nine)
    grad_k, grad_v = call(
        functools.partial(last_kernel, blocks),
        "last",
        [bf16((rows, width)), bf16((rows, width))],
        [where, marks],
        [packed, part_k, part_v, *two_spans(nine, True)],
        4 * rows * width * HEAD_DIM,
    )
    return normed.transpose(1, 0, 2).reshape(tokens, cols), grad_q, grad_k, grad_v


def solution(mesh):
    placed = P(("seq", "head"), None)
    return jax.shard_map(
        on_device,
        mesh=mesh,
        in_specs=(placed, placed, placed, placed, P(), P()),
        out_specs=(placed, P("seq", "head"), P("seq", "head"), P("seq", "head")),
        check_vma=False,
    )
```

```python
import functools

import jax
import jax.numpy as jnp
from jax import lax
from jax.experimental import pallas as pl
from jax.experimental.pallas import tpu as pltpu
from jax.sharding import PartitionSpec as P

HEAD_DIM = 128
TILE = 256


epsilon = 1e-05

F32 = jnp.float32
BF16 = jnp.bfloat16

ROWS = (((0,), (0,)), ((), ()))
FEATURES = (((1,), (1,)), ((), ()))
PLAIN = (((1,), (0,)), ((), ()))


def dot(a, b, dims):
    return lax.dot_general(a, b, dims, preferred_element_type=F32)


def unpacked(packed_ref, at):
    groups, stacked, width = packed_ref.shape
    tokens = stacked // 4
    return packed_ref[:, at * tokens : (at + 1) * tokens, :].reshape(groups * tokens, width)


def head_cols(head):
    return slice(head * HEAD_DIM, (head + 1) * HEAD_DIM)


def meta_kernel(blocks, rows, lengths_ref, where_ref, marks_ref):
    first = where_ref[0] * rows
    last = first + rows - 1

    def clear(i, carry):
        marks_ref[i] = 0
        return carry

    lax.fori_loop(0, 2 * blocks, clear, 0)
    marks_ref[2 * blocks - 1] = 1
    marks_ref[2 * blocks + 1] = 0
    marks_ref[2 * blocks + 3] = rows

    def step(i, begin):
        after = begin + lengths_ref[i]
        marks_ref[begin // rows] = 1
        marks_ref[blocks + jnp.maximum(begin - 1, 0) // rows] = 1

        @pl.when((begin <= first) & (first < after))
        def _():
            marks_ref[2 * blocks] = after - first
            marks_ref[2 * blocks + 1] = jnp.where(begin < first, after - first, 0)

        @pl.when((begin <= last) & (last < after))
        def _():
            marks_ref[2 * blocks + 2] = begin - first
            marks_ref[2 * blocks + 3] = jnp.where(after > last + 1, begin - first, rows)

        return after

    lax.fori_loop(0, lengths_ref.shape[0], step, jnp.int32(0))


def docs_kernel(lengths_ref, where_ref, marks_ref, span_ref):
    rows = span_ref.shape[1]
    first = where_ref[0] * rows
    place = first + lax.broadcasted_iota(jnp.int32, (1, rows), 1)

    def step(i, carry):
        begin, start, end = carry
        after = begin + lengths_ref[i]
        inside = (place >= begin) & (place < after)
        return (after, jnp.where(inside, begin, start), jnp.where(inside, after, end))

    zero = jnp.zeros((1, rows), jnp.int32)
    _, start, end = lax.fori_loop(0, lengths_ref.shape[0], step, (jnp.int32(0), zero, zero))
    span_ref[0:1, :] = start - first
    span_ref[1:2, :] = end - first


def pack_kernel(*refs):
    *arrays, ended_ref, out_ref, held, in_sems, out_sems = refs
    ended_ref[...] = jnp.zeros_like(ended_ref)
    groups, _, width = out_ref.shape
    tokens = arrays[0].shape[0]
    inward = [
        pltpu.make_async_copy(ref, held.at[k], in_sems.at[k]) for k, ref in enumerate(arrays)
    ]
    outward = [
        [
            pltpu.make_async_copy(
                held.at[k, :, pl.ds(at * width, width)],
                out_ref.at[at, pl.ds(k * tokens, tokens), :],
                out_sems.at[k, at],
            )
            for at in range(groups)
        ]
        for k in range(len(arrays))
    ]
    for copy in inward:
        copy.start()
    for copy, parts in zip(inward, outward):
        copy.wait()
        for part in parts:
            part.start()
    for parts in outward:
        for part in parts:
            part.wait()


def parts_kernel(lengths_ref, seq_ref, head_ref, keys_ref, values_ref, ended_ref, out_ref, held, sems):
    copies = [
        pltpu.make_async_copy(ref, held.at[k], sems.at[k])
        for k, ref in enumerate((keys_ref, values_ref))
    ]
    for copy in copies:
        copy.start()
    ended_ref[...] = jnp.zeros_like(ended_ref)
    groups, width, _ = out_ref.shape
    tokens, cols = keys_ref.shape
    last = (seq_ref[0] + 1) * (tokens * groups) - 1
    begin, bound = jnp.int32(0), jnp.int32(0)
    for i in range(lengths_ref.shape[0]):
        bound = jnp.where(begin <= last, begin, bound)
        begin = begin + lengths_ref[i]
    mine = last + 1 - (groups - head_ref[0]) * tokens
    for copy in copies:
        copy.wait()
    place = mine + lax.broadcasted_iota(jnp.int32, (tokens, cols), 0)
    keys = held[0]
    keys = jnp.where(place >= bound, keys, jnp.zeros_like(keys))
    for head in range(cols // HEAD_DIM):
        part = dot(keys[:, head_cols(head)], held[1, :, head_cols(head)], ROWS)
        group, at = divmod(head * HEAD_DIM, width)
        out_ref[group, at : at + HEAD_DIM, :] = part.astype(out_ref.dtype)


def tail_kernel(marks_ref, parts_ref, tail_ref):
    total = parts_ref[0].astype(F32)
    for k in range(1, parts_ref.shape[0]):
        total = total + parts_ref[k].astype(F32)
    tail_ref[...] = total.astype(tail_ref.dtype)


def block_mark(marks_ref, blocks, at, reverse):
    return marks_ref[lax.rem(at + blocks, blocks) + (blocks if reverse else 0)]


def chained(reverse, blocks, where_ref, marks_ref, refs, covers):
    mine, sign = where_ref[0], -1 if reverse else 1
    total = refs[0][...].astype(F32)
    for ref, (low, high) in zip(refs[1:], covers[1:]):
        mark = jnp.int32(0)
        for at in range(low, high + 1):
            mark = jnp.maximum(mark, block_mark(marks_ref, blocks, mine + sign * at, reverse))
        total = jnp.where(mark > 0, 0.0, total) + ref[...].astype(F32)
    return total.astype(BF16)


def three_kernel(reverse, blocks, where_ref, marks_ref, *refs):
    *parts, span_ref = refs
    covers = ((-1, -1), (0, 0), (1, 1))
    span_ref[...] = chained(reverse, blocks, where_ref, marks_ref, parts, covers)


def nine_kernel(reverse, blocks, where_ref, marks_ref, *refs):
    *parts, span_ref = refs
    covers = ((-4, -2), (-1, 1), (2, 4))
    span_ref[...] = chained(reverse, blocks, where_ref, marks_ref, parts, covers)


def entering(reverse, blocks, where_ref, marks_ref, *refs):
    return chained(reverse, blocks, where_ref, marks_ref, refs, ((-18, -10), (-9, -1)))


def intra_kernel(span_ref, packed_ref, intra_ref):
    keys, values, queries = (unpacked(packed_ref, at) for at in range(3))
    rows, width = keys.shape
    for low in range(0, rows, TILE):
        high = low + TILE
        row = low + lax.broadcasted_iota(jnp.int32, (TILE, high), 0)
        column = lax.broadcasted_iota(jnp.int32, (TILE, high), 1)
        mask = (column <= row) & (row < span_ref[1:2, :high])
        for head in range(width // HEAD_DIM):
            cols = head_cols(head)
            scores = dot(queries[low:high, cols], keys[:high, cols], FEATURES)
            attn = jnp.where(mask, scores, 0.0).astype(BF16)
            intra_ref[low:high, cols] = dot(attn, values[:high, cols], PLAIN)


def norm_kernel(blocks, where_ref, marks_ref, packed_ref, intra_ref, gain_ref, *refs):
    far_ref, near_ref, normed_ref, grad_ref, part_ref, state_ref = refs
    queries, cotangent = unpacked(packed_ref, 2), unpacked(packed_ref, 3)
    state = entering(False, blocks, where_ref, marks_ref, far_ref, near_ref)
    state_ref[...] = state
    rows, width = intra_ref.shape
    tile = HEAD_DIM
    for head in range(width // HEAD_DIM):
        cols = head_cols(head)
        at = pl.multiple_of(where_ref[1] * width + head * HEAD_DIM, HEAD_DIM)
        gain = gain_ref[:, pl.ds(at, HEAD_DIM)]
        for low in range(0, rows, tile):
            here = slice(low, low + tile)
            place = low + lax.broadcasted_iota(jnp.int32, (tile, HEAD_DIM), 0)
            inter = dot(queries[here, cols], state[cols, :], PLAIN)
            inter = jnp.where(place < marks_ref[2 * blocks + 1], inter, 0.0)
            attended = intra_ref[here, cols] + inter
            scale = lax.rsqrt(jnp.mean(attended * attended, axis=-1, keepdims=True) + epsilon)
            unit = attended * scale
            normed_ref[here, cols] = (unit * gain).astype(BF16)
            pulled = cotangent[here, cols].astype(F32) * gain
            along = jnp.mean(pulled * unit, axis=-1, keepdims=True)
            grad_ref[here, cols] = (scale * (pulled - unit * along)).astype(BF16)
    place = lax.broadcasted_iota(jnp.int32, (rows, HEAD_DIM), 0)
    in_first = place < marks_ref[2 * blocks]
    for head in range(width // HEAD_DIM):
        cols = head_cols(head)
        q = queries[:, cols]
        kept = jnp.where(in_first, q, jnp.zeros_like(q))
        part_ref[cols, :] = dot(kept, grad_ref[:, cols], ROWS).astype(part_ref.dtype)


def grad_q_kernel(blocks, marks_ref, span_ref, packed_ref, grad_ref, state_ref, ended_ref, grad_q_ref):
    ended_ref[...] = jnp.zeros_like(ended_ref)
    keys, values = unpacked(packed_ref, 0), unpacked(packed_ref, 1)
    rows, width = keys.shape
    for low in range(0, rows, TILE):
        high = low + TILE
        row = low + lax.broadcasted_iota(jnp.int32, (TILE, high), 0)
        column = lax.broadcasted_iota(jnp.int32, (TILE, high), 1)
        mask = (column <= row) & (row < span_ref[1:2, :high])
        place = low + lax.broadcasted_iota(jnp.int32, (TILE, HEAD_DIM), 0)
        carried = place < marks_ref[2 * blocks + 1]
        for head in range(width // HEAD_DIM):
            cols = head_cols(head)
            grad = grad_ref[low:high, cols]
            scores = dot(grad, values[:high, cols], FEATURES)
            grad_attn = jnp.where(mask, scores, 0.0).astype(BF16)
            inter = dot(grad, state_ref[cols, :], FEATURES)
            grad_q = dot(grad_attn, keys[:high, cols], PLAIN) + jnp.where(carried, inter, 0.0)
            grad_q_ref[low:high, cols] = grad_q.astype(BF16)


def turned_kernel(docs_ref, left_ref, right_ref, rows_ref, part_ref):
    left, right, summed = (
        unpacked(*field) if isinstance(field, tuple) else field for field in (left_ref, right_ref, rows_ref)
    )
    rows, width = part_ref.shape
    for low in range(0, rows, TILE):
        high = low + TILE
        row = low + lax.broadcasted_iota(jnp.int32, (TILE, rows - low), 0)
        column = low + lax.broadcasted_iota(jnp.int32, (TILE, rows - low), 1)
        mask = (row <= column) & (row >= docs_ref[0:1, low:])
        for head in range(width // HEAD_DIM):
            cols = head_cols(head)
            turned = dot(left[low:high, cols], right[low:, cols], FEATURES)
            turned = jnp.where(mask, turned, 0.0).astype(BF16)
            part_ref[low:high, cols] = dot(turned, summed[low:, cols], PLAIN)


def grad_k_kernel(docs_ref, packed_ref, grad_ref, ended_ref, part_ref):
    ended_ref[...] = jnp.zeros_like(ended_ref)
    turned_kernel(docs_ref, (packed_ref, 1), grad_ref, (packed_ref, 2), part_ref)


def grad_v_kernel(docs_ref, packed_ref, grad_ref, part_ref):
    turned_kernel(docs_ref, (packed_ref, 0), (packed_ref, 2), grad_ref, part_ref)


def last_kernel(
    blocks, where_ref, marks_ref, packed_ref, part_k_ref, part_v_ref, far_ref, near_ref, grad_k_ref, grad_v_ref
):
    keys, values = unpacked(packed_ref, 0), unpacked(packed_ref, 1)
    back = entering(True, blocks, where_ref, marks_ref, far_ref, near_ref)
    rows, width = keys.shape
    place = lax.broadcasted_iota(jnp.int32, (rows, HEAD_DIM), 0)
    later = place >= marks_ref[2 * blocks + 3]
    for head in range(width // HEAD_DIM):
        cols = head_cols(head)
        inter = dot(values[:, cols], back[cols, :], FEATURES)
        grad_k_ref[:, cols] = (part_k_ref[:, cols] + jnp.where(later, inter, 0.0)).astype(BF16)
        inter = dot(keys[:, cols], back[cols, :], PLAIN)
        grad_v_ref[:, cols] = (part_v_ref[:, cols] + jnp.where(later, inter, 0.0)).astype(BF16)


SMEM = pl.BlockSpec(memory_space=pltpu.SMEM)
VMEM = pl.BlockSpec(memory_space=pltpu.VMEM)
ANYWHERE = pl.BlockSpec(memory_space=pl.ANY)
ENDED = jax.ShapeDtypeStruct((8, HEAD_DIM), F32)


def call(
    kernel, name, outs, scalars, arrays, flops, scratch=(), after=(), in_specs=None, out_specs=None, limit=40, aliases=None
):
    moved = sum(a.size * a.dtype.itemsize for a in (*arrays, *outs))
    given = len(scalars) + len(arrays)

    def body(*refs):
        kernel(*refs[:given], *refs[given + len(after) :])

    return pl.pallas_call(
        body,
        name=name,
        out_shape=outs,
        in_specs=[SMEM] * len(scalars) + (in_specs or [VMEM] * len(arrays)) + [ANYWHERE] * len(after),
        out_specs=out_specs or [VMEM] * len(outs),
        scratch_shapes=list(scratch),
        input_output_aliases=aliases or {},
        compiler_params=pltpu.CompilerParams(vmem_limit_bytes=limit * 1024 * 1024),
        cost_estimate=pl.CostEstimate(flops=flops, bytes_accessed=moved, transcendentals=0),
    )(*scalars, *arrays, *after)


def across_head(parts):
    return lax.all_to_all(parts, "head", split_axis=0, concat_axis=0, tiled=True)


def to_heads(arrays, after):
    groups, count = lax.axis_size("head"), len(arrays)
    tokens, cols = arrays[0].shape
    ended, packed = call(
        pack_kernel,
        "pack",
        [ENDED, jax.ShapeDtypeStruct((groups, count * tokens, cols // groups), BF16)],
        [],
        arrays,
        0,
        [
            pltpu.VMEM((count, tokens, cols), BF16),
            pltpu.SemaphoreType.DMA((count,)),
            pltpu.SemaphoreType.DMA((count, groups)),
        ],
        after,
        [ANYWHERE] * count,
        [VMEM, ANYWHERE],
        60,
    )
    return ended, packed


def from_block(field, step, reach, reverse):
    blocks = lax.axis_size("seq")
    pairs = []
    for at in range(blocks):
        to = at + step
        if to < blocks or to - blocks - step + reach >= 0:
            pairs.append((at, to % blocks))
    if reverse:
        pairs = [(blocks - 1 - at, blocks - 1 - to) for at, to in pairs]
    return lax.ppermute(field, "seq", pairs)


def span(kernel, parts, where, marks, reverse, after=()):
    blocks = lax.axis_size("seq")
    return call(
        functools.partial(kernel, reverse, blocks),
        kernel.__name__.replace("kernel", "back" if reverse else "forward"),
        [jax.ShapeDtypeStruct(parts[0].shape, BF16)],
        [where, marks],
        parts,
        len(parts) * parts[0].size,
        after=after,
    )[0]


def span_of_three(part, where, marks, reverse, after=()):
    parts = [from_block(part, 1, 0, reverse), part, from_block(part, -1, 0, reverse)]
    return span(three_kernel, parts, where, marks, reverse, after)


def span_of_nine(three, where, marks, reverse, after=()):
    parts = [from_block(three, 3, 1, reverse), three, from_block(three, -3, 1, reverse)]
    return span(nine_kernel, parts, where, marks, reverse, after)


def two_spans(nine, reverse):
    return [from_block(nine, 14, 4, reverse), from_block(nine, 5, 4, reverse)]


def on_device(queries, keys, values, cotangent, gain, lengths):
    groups, blocks = lax.axis_size("head"), lax.axis_size("seq")
    tokens, cols = queries.shape
    rows, width = tokens * groups, cols // groups
    square = rows * rows * width
    here = lax.axis_index("head").astype(jnp.int32)
    where = jnp.stack([lax.axis_index("seq").astype(jnp.int32), here])
    f32 = functools.partial(jax.ShapeDtypeStruct, dtype=F32)
    bf16 = functools.partial(jax.ShapeDtypeStruct, dtype=BF16)
    int32 = functools.partial(jax.ShapeDtypeStruct, dtype=jnp.int32)
    started, parts = call(
        parts_kernel,
        "parts",
        [ENDED, bf16((groups, width, HEAD_DIM))],
        [lengths, lax.axis_index("seq").astype(jnp.int32).reshape(1), here.reshape(1)],
        [keys, values],
        2 * tokens * cols * HEAD_DIM,
        [
            pltpu.VMEM((2, tokens, cols), BF16),
            pltpu.SemaphoreType.DMA((2,)),
        ],
        in_specs=[ANYWHERE] * 2,
        limit=60,
    )
    (marks,) = call(
        functools.partial(meta_kernel, blocks, rows),
        "meta",
        [int32((2 * blocks + 4,))],
        [lengths, where],
        [],
        rows,
        after=[started],
        out_specs=[SMEM],
    )
    (docs,) = call(docs_kernel, "docs", [int32((2, rows))], [lengths, where, marks], [], rows)
    gathered = across_head(parts)
    ended, packed = to_heads([keys, values, queries, cotangent], [docs])
    (tail,) = call(
        tail_kernel,
        "tail",
        [bf16((width, HEAD_DIM))],
        [marks],
        [gathered],
        gathered.size,
        after=[ended],
    )
    packed = across_head(packed)
    three = span_of_three(tail, where, marks, False)
    before = two_spans(span_of_nine(three, where, marks, False), False)
    (inside,) = call(intra_kernel, "intra", [f32((rows, width))], [], [docs, packed], 2 * square)
    normed, grad, part, state = call(
        functools.partial(norm_kernel, blocks),
        "norm",
        [bf16((rows, width)), bf16((rows, width)), bf16((width, HEAD_DIM)), bf16((width, HEAD_DIM))],
        [where, marks],
        [packed, inside, gain.reshape(1, cols), *before],
        4 * rows * width * HEAD_DIM,
    )

    normed = across_head(normed.reshape(groups, tokens, width))
    ended, part_k = call(
        grad_k_kernel, "grads_k", [ENDED, f32((rows, width))], [], [docs, packed, grad], 2 * square
    )
    three = span_of_three(part, where, marks, True, [ended])
    ended, grad_q = call(
        functools.partial(grad_q_kernel, blocks),
        "grads_q",
        [ENDED, bf16((rows, width))],
        [marks],
        [docs, packed, grad, state],
        2 * square,
        after=[three],
    )
    nine = span_of_nine(three, where, marks, True, [ended])
    (part_v,) = call(
        grad_v_kernel, "grads_v", [f32((rows, width))], [], [docs, packed, grad], 2 * square, after=[nine]
    )
    grad_k, grad_v = call(
        functools.partial(last_kernel, blocks),
        "last",
        [bf16((rows, width)), bf16((rows, width))],
        [where, marks],
        [packed, part_k, part_v, *two_spans(nine, True)],
        4 * rows * width * HEAD_DIM,
    )
    return normed.transpose(1, 0, 2).reshape(tokens, cols), grad_q, grad_k, grad_v


def solution(mesh):
    placed = P(("seq", "head"), None)
    return jax.shard_map(
        on_device,
        mesh=mesh,
        in_specs=(placed, placed, placed, placed, P(), P()),
        out_specs=(placed, P("seq", "head"), P("seq", "head"), P("seq", "head")),
        check_vma=False,
    )
```

```python
import functools

import jax
import jax.numpy as jnp
from jax import lax
from jax.experimental import pallas as pl
from jax.experimental.pallas import tpu as pltpu
from jax.sharding import PartitionSpec as P

HEAD_DIM = 128
TILE = 256


epsilon = 1e-05

F32 = jnp.float32
BF16 = jnp.bfloat16

ROWS = (((0,), (0,)), ((), ()))
FEATURES = (((1,), (1,)), ((), ()))
PLAIN = (((1,), (0,)), ((), ()))


def dot(a, b, dims):
    return lax.dot_general(a, b, dims, preferred_element_type=F32)


def unpacked(packed_ref, at):
    groups, stacked, width = packed_ref.shape
    tokens = stacked // 4
    return packed_ref[:, at * tokens : (at + 1) * tokens, :].reshape(groups * tokens, width)


def head_cols(head):
    return slice(head * HEAD_DIM, (head + 1) * HEAD_DIM)


def meta_kernel(blocks, rows, lengths_ref, where_ref, marks_ref):
    first = where_ref[0] * rows
    last = first + rows - 1

    def clear(i, carry):
        marks_ref[i] = 0
        return carry

    lax.fori_loop(0, 2 * blocks, clear, 0)
    marks_ref[2 * blocks - 1] = 1
    marks_ref[2 * blocks + 1] = 0
    marks_ref[2 * blocks + 3] = rows

    def step(i, begin):
        after = begin + lengths_ref[i]
        marks_ref[begin // rows] = 1
        marks_ref[blocks + jnp.maximum(begin - 1, 0) // rows] = 1

        @pl.when((begin <= first) & (first < after))
        def _():
            marks_ref[2 * blocks] = after - first
            marks_ref[2 * blocks + 1] = jnp.where(begin < first, after - first, 0)

        @pl.when((begin <= last) & (last < after))
        def _():
            marks_ref[2 * blocks + 2] = begin - first
            marks_ref[2 * blocks + 3] = jnp.where(after > last + 1, begin - first, rows)

        return after

    lax.fori_loop(0, lengths_ref.shape[0], step, jnp.int32(0))


def docs_kernel(lengths_ref, where_ref, marks_ref, span_ref):
    rows = span_ref.shape[1]
    first = where_ref[0] * rows
    place = first + lax.broadcasted_iota(jnp.int32, (1, rows), 1)

    def step(i, carry):
        begin, start, end = carry
        after = begin + lengths_ref[i]
        inside = (place >= begin) & (place < after)
        return (after, jnp.where(inside, begin, start), jnp.where(inside, after, end))

    zero = jnp.zeros((1, rows), jnp.int32)
    _, start, end = lax.fori_loop(0, lengths_ref.shape[0], step, (jnp.int32(0), zero, zero))
    span_ref[0:1, :] = start - first
    span_ref[1:2, :] = end - first


def pack_kernel(*refs):
    *arrays, ended_ref, out_ref, held, in_sems, out_sems = refs
    ended_ref[...] = jnp.zeros_like(ended_ref)
    groups, _, width = out_ref.shape
    tokens = arrays[0].shape[0]
    inward = [
        pltpu.make_async_copy(ref, held.at[k], in_sems.at[k]) for k, ref in enumerate(arrays)
    ]
    outward = [
        [
            pltpu.make_async_copy(
                held.at[k, :, pl.ds(at * width, width)],
                out_ref.at[at, pl.ds(k * tokens, tokens), :],
                out_sems.at[k, at],
            )
            for at in range(groups)
        ]
        for k in range(len(arrays))
    ]
    for copy in inward:
        copy.start()
    for copy, parts in zip(inward, outward):
        copy.wait()
        for part in parts:
            part.start()
    for parts in outward:
        for part in parts:
            part.wait()


def parts_kernel(lengths_ref, seq_ref, head_ref, keys_ref, values_ref, ended_ref, out_ref, held, sems):
    copies = [
        pltpu.make_async_copy(ref, held.at[k], sems.at[k])
        for k, ref in enumerate((keys_ref, values_ref))
    ]
    for copy in copies:
        copy.start()
    ended_ref[...] = jnp.zeros_like(ended_ref)
    groups, width, _ = out_ref.shape
    tokens, cols = keys_ref.shape
    last = (seq_ref[0] + 1) * (tokens * groups) - 1
    begin, bound = jnp.int32(0), jnp.int32(0)
    for i in range(lengths_ref.shape[0]):
        bound = jnp.where(begin <= last, begin, bound)
        begin = begin + lengths_ref[i]
    mine = last + 1 - (groups - head_ref[0]) * tokens
    for copy in copies:
        copy.wait()
    place = mine + lax.broadcasted_iota(jnp.int32, (tokens, cols), 0)
    keys = held[0]
    keys = jnp.where(place >= bound, keys, jnp.zeros_like(keys))
    for head in range(cols // HEAD_DIM):
        part = dot(keys[:, head_cols(head)], held[1, :, head_cols(head)], ROWS)
        group, at = divmod(head * HEAD_DIM, width)
        out_ref[group, at : at + HEAD_DIM, :] = part.astype(out_ref.dtype)


def tail_kernel(marks_ref, parts_ref, tail_ref):
    total = parts_ref[0].astype(F32)
    for k in range(1, parts_ref.shape[0]):
        total = total + parts_ref[k].astype(F32)
    tail_ref[...] = total.astype(tail_ref.dtype)


def block_mark(marks_ref, blocks, at, reverse):
    return marks_ref[lax.rem(at + blocks, blocks) + (blocks if reverse else 0)]


def chained(reverse, blocks, where_ref, marks_ref, refs, covers):
    mine, sign = where_ref[0], -1 if reverse else 1
    total = refs[0][...].astype(F32)
    for ref, (low, high) in zip(refs[1:], covers[1:]):
        mark = jnp.int32(0)
        for at in range(low, high + 1):
            mark = jnp.maximum(mark, block_mark(marks_ref, blocks, mine + sign * at, reverse))
        total = jnp.where(mark > 0, 0.0, total) + ref[...].astype(F32)
    return total.astype(BF16)


def three_kernel(reverse, blocks, where_ref, marks_ref, *refs):
    *parts, span_ref = refs
    covers = ((-1, -1), (0, 0), (1, 1))
    span_ref[...] = chained(reverse, blocks, where_ref, marks_ref, parts, covers)


def nine_kernel(reverse, blocks, where_ref, marks_ref, *refs):
    *parts, span_ref = refs
    covers = ((-4, -2), (-1, 1), (2, 4))
    span_ref[...] = chained(reverse, blocks, where_ref, marks_ref, parts, covers)


def entering(reverse, blocks, where_ref, marks_ref, *refs):
    return chained(reverse, blocks, where_ref, marks_ref, refs, ((-18, -10), (-9, -1)))


def intra_kernel(span_ref, packed_ref, intra_ref):
    keys, values, queries = (unpacked(packed_ref, at) for at in range(3))
    rows, width = keys.shape
    for low in range(0, rows, TILE):
        high = low + TILE
        row = low + lax.broadcasted_iota(jnp.int32, (TILE, high), 0)
        column = lax.broadcasted_iota(jnp.int32, (TILE, high), 1)
        mask = (column <= row) & (row < span_ref[1:2, :high])
        for head in range(width // HEAD_DIM):
            cols = head_cols(head)
            scores = dot(queries[low:high, cols], keys[:high, cols], FEATURES)
            attn = jnp.where(mask, scores, 0.0).astype(BF16)
            intra_ref[low:high, cols] = dot(attn, values[:high, cols], PLAIN)


def norm_kernel(blocks, where_ref, marks_ref, packed_ref, intra_ref, gain_ref, *refs):
    far_ref, near_ref, normed_ref, grad_ref, part_ref, state_ref = refs
    queries, cotangent = unpacked(packed_ref, 2), unpacked(packed_ref, 3)
    state = entering(False, blocks, where_ref, marks_ref, far_ref, near_ref)
    state_ref[...] = state
    rows, width = intra_ref.shape
    tile = HEAD_DIM
    for head in range(width // HEAD_DIM):
        cols = head_cols(head)
        at = pl.multiple_of(where_ref[1] * width + head * HEAD_DIM, HEAD_DIM)
        gain = gain_ref[:, pl.ds(at, HEAD_DIM)]
        for low in range(0, rows, tile):
            here = slice(low, low + tile)
            place = low + lax.broadcasted_iota(jnp.int32, (tile, HEAD_DIM), 0)
            inter = dot(queries[here, cols], state[cols, :], PLAIN)
            inter = jnp.where(place < marks_ref[2 * blocks + 1], inter, 0.0)
            attended = intra_ref[here, cols] + inter
            scale = lax.rsqrt(jnp.mean(attended * attended, axis=-1, keepdims=True) + epsilon)
            unit = attended * scale
            normed_ref[here, cols] = (unit * gain).astype(BF16)
            pulled = cotangent[here, cols].astype(F32) * gain
            along = jnp.mean(pulled * unit, axis=-1, keepdims=True)
            grad_ref[here, cols] = (scale * (pulled - unit * along)).astype(BF16)
    place = lax.broadcasted_iota(jnp.int32, (rows, HEAD_DIM), 0)
    in_first = place < marks_ref[2 * blocks]
    for head in range(width // HEAD_DIM):
        cols = head_cols(head)
        q = queries[:, cols]
        kept = jnp.where(in_first, q, jnp.zeros_like(q))
        part_ref[cols, :] = dot(kept, grad_ref[:, cols], ROWS).astype(part_ref.dtype)


def grad_q_kernel(blocks, marks_ref, span_ref, packed_ref, grad_ref, state_ref, ended_ref, grad_q_ref):
    ended_ref[...] = jnp.zeros_like(ended_ref)
    keys, values = unpacked(packed_ref, 0), unpacked(packed_ref, 1)
    rows, width = keys.shape
    for low in range(0, rows, TILE):
        high = low + TILE
        row = low + lax.broadcasted_iota(jnp.int32, (TILE, high), 0)
        column = lax.broadcasted_iota(jnp.int32, (TILE, high), 1)
        mask = (column <= row) & (row < span_ref[1:2, :high])
        place = low + lax.broadcasted_iota(jnp.int32, (TILE, HEAD_DIM), 0)
        carried = place < marks_ref[2 * blocks + 1]
        for head in range(width // HEAD_DIM):
            cols = head_cols(head)
            grad = grad_ref[low:high, cols]
            scores = dot(grad, values[:high, cols], FEATURES)
            grad_attn = jnp.where(mask, scores, 0.0).astype(BF16)
            inter = dot(grad, state_ref[cols, :], FEATURES)
            grad_q = dot(grad_attn, keys[:high, cols], PLAIN) + jnp.where(carried, inter, 0.0)
            grad_q_ref[low:high, cols] = grad_q.astype(BF16)


def grad_kv_kernel(docs_ref, packed_ref, grad_ref, ended_ref, part_k_ref, part_v_ref):
    ended_ref[...] = jnp.zeros_like(ended_ref)
    keys, values, queries = (unpacked(packed_ref, at) for at in range(3))
    rows, width = keys.shape
    for low in range(0, rows, TILE):
        high = low + TILE
        row = low + lax.broadcasted_iota(jnp.int32, (TILE, rows - low), 0)
        column = low + lax.broadcasted_iota(jnp.int32, (TILE, rows - low), 1)
        mask = (row <= column) & (row >= docs_ref[0:1, low:])
        for head in range(width // HEAD_DIM):
            cols = head_cols(head)
            q, k, v = (field[:, cols] for field in (queries, keys, values))
            grad = grad_ref[:, cols]
            turned = dot(v[low:high], grad[low:], FEATURES)
            turned = jnp.where(mask, turned, 0.0).astype(BF16)
            part_k_ref[low:high, cols] = dot(turned, q[low:], PLAIN)
            turned = dot(k[low:high], q[low:], FEATURES)
            turned = jnp.where(mask, turned, 0.0).astype(BF16)
            part_v_ref[low:high, cols] = dot(turned, grad[low:], PLAIN)


def last_kernel(
    blocks, where_ref, marks_ref, packed_ref, part_k_ref, part_v_ref, far_ref, near_ref, grad_k_ref, grad_v_ref
):
    keys, values = unpacked(packed_ref, 0), unpacked(packed_ref, 1)
    back = entering(True, blocks, where_ref, marks_ref, far_ref, near_ref)
    rows, width = keys.shape
    place = lax.broadcasted_iota(jnp.int32, (rows, HEAD_DIM), 0)
    later = place >= marks_ref[2 * blocks + 3]
    for head in range(width // HEAD_DIM):
        cols = head_cols(head)
        inter = dot(values[:, cols], back[cols, :], FEATURES)
        grad_k_ref[:, cols] = (part_k_ref[:, cols] + jnp.where(later, inter, 0.0)).astype(BF16)
        inter = dot(keys[:, cols], back[cols, :], PLAIN)
        grad_v_ref[:, cols] = (part_v_ref[:, cols] + jnp.where(later, inter, 0.0)).astype(BF16)


SMEM = pl.BlockSpec(memory_space=pltpu.SMEM)
VMEM = pl.BlockSpec(memory_space=pltpu.VMEM)
ANYWHERE = pl.BlockSpec(memory_space=pl.ANY)
ENDED = jax.ShapeDtypeStruct((8, HEAD_DIM), F32)


def call(
    kernel, name, outs, scalars, arrays, flops, scratch=(), after=(), in_specs=None, out_specs=None, limit=40, aliases=None
):
    moved = sum(a.size * a.dtype.itemsize for a in (*arrays, *outs))
    given = len(scalars) + len(arrays)

    def body(*refs):
        kernel(*refs[:given], *refs[given + len(after) :])

    return pl.pallas_call(
        body,
        name=name,
        out_shape=outs,
        in_specs=[SMEM] * len(scalars) + (in_specs or [VMEM] * len(arrays)) + [ANYWHERE] * len(after),
        out_specs=out_specs or [VMEM] * len(outs),
        scratch_shapes=list(scratch),
        input_output_aliases=aliases or {},
        compiler_params=pltpu.CompilerParams(vmem_limit_bytes=limit * 1024 * 1024),
        cost_estimate=pl.CostEstimate(flops=flops, bytes_accessed=moved, transcendentals=0),
    )(*scalars, *arrays, *after)


def across_head(parts):
    return lax.all_to_all(parts, "head", split_axis=0, concat_axis=0, tiled=True)


def to_heads(arrays, after):
    groups, count = lax.axis_size("head"), len(arrays)
    tokens, cols = arrays[0].shape
    ended, packed = call(
        pack_kernel,
        "pack",
        [ENDED, jax.ShapeDtypeStruct((groups, count * tokens, cols // groups), BF16)],
        [],
        arrays,
        0,
        [
            pltpu.VMEM((count, tokens, cols), BF16),
            pltpu.SemaphoreType.DMA((count,)),
            pltpu.SemaphoreType.DMA((count, groups)),
        ],
        after,
        [ANYWHERE] * count,
        [VMEM, ANYWHERE],
        60,
    )
    return ended, packed


def from_block(field, step, reach, reverse):
    blocks = lax.axis_size("seq")
    pairs = []
    for at in range(blocks):
        to = at + step
        if to < blocks or to - blocks - step + reach >= 0:
            pairs.append((at, to % blocks))
    if reverse:
        pairs = [(blocks - 1 - at, blocks - 1 - to) for at, to in pairs]
    return lax.ppermute(field, "seq", pairs)


def span(kernel, parts, where, marks, reverse, after=()):
    blocks = lax.axis_size("seq")
    return call(
        functools.partial(kernel, reverse, blocks),
        kernel.__name__.replace("kernel", "back" if reverse else "forward"),
        [jax.ShapeDtypeStruct(parts[0].shape, BF16)],
        [where, marks],
        parts,
        len(parts) * parts[0].size,
        after=after,
    )[0]


def span_of_three(part, where, marks, reverse, after=()):
    parts = [from_block(part, 1, 0, reverse), part, from_block(part, -1, 0, reverse)]
    return span(three_kernel, parts, where, marks, reverse, after)


def span_of_nine(three, where, marks, reverse, after=()):
    parts = [from_block(three, 3, 1, reverse), three, from_block(three, -3, 1, reverse)]
    return span(nine_kernel, parts, where, marks, reverse, after)


def two_spans(nine, reverse):
    return [from_block(nine, 14, 4, reverse), from_block(nine, 5, 4, reverse)]


def on_device(queries, keys, values, cotangent, gain, lengths):
    groups, blocks = lax.axis_size("head"), lax.axis_size("seq")
    tokens, cols = queries.shape
    rows, width = tokens * groups, cols // groups
    square = rows * rows * width
    here = lax.axis_index("head").astype(jnp.int32)
    where = jnp.stack([lax.axis_index("seq").astype(jnp.int32), here])
    f32 = functools.partial(jax.ShapeDtypeStruct, dtype=F32)
    bf16 = functools.partial(jax.ShapeDtypeStruct, dtype=BF16)
    int32 = functools.partial(jax.ShapeDtypeStruct, dtype=jnp.int32)
    started, parts = call(
        parts_kernel,
        "parts",
        [ENDED, bf16((groups, width, HEAD_DIM))],
        [lengths, lax.axis_index("seq").astype(jnp.int32).reshape(1), here.reshape(1)],
        [keys, values],
        2 * tokens * cols * HEAD_DIM,
        [
            pltpu.VMEM((2, tokens, cols), BF16),
            pltpu.SemaphoreType.DMA((2,)),
        ],
        in_specs=[ANYWHERE] * 2,
        limit=60,
    )
    (marks,) = call(
        functools.partial(meta_kernel, blocks, rows),
        "meta",
        [int32((2 * blocks + 4,))],
        [lengths, where],
        [],
        rows,
        after=[started],
        out_specs=[SMEM],
    )
    (docs,) = call(docs_kernel, "docs", [int32((2, rows))], [lengths, where, marks], [], rows)
    gathered = across_head(parts)
    ended, packed = to_heads([keys, values, queries, cotangent], [docs])
    (tail,) = call(
        tail_kernel,
        "tail",
        [bf16((width, HEAD_DIM))],
        [marks],
        [gathered],
        gathered.size,
        after=[ended],
    )
    packed = across_head(packed)
    three = span_of_three(tail, where, marks, False)
    before = two_spans(span_of_nine(three, where, marks, False), False)
    (inside,) = call(intra_kernel, "intra", [f32((rows, width))], [], [docs, packed], 2 * square)
    normed, grad, part, state = call(
        functools.partial(norm_kernel, blocks),
        "norm",
        [bf16((rows, width)), bf16((rows, width)), bf16((width, HEAD_DIM)), bf16((width, HEAD_DIM))],
        [where, marks],
        [packed, inside, gain.reshape(1, cols), *before],
        4 * rows * width * HEAD_DIM,
    )

    normed = across_head(normed.reshape(groups, tokens, width))
    ended, part_k, part_v = call(
        grad_kv_kernel,
        "grads_kv",
        [ENDED, f32((rows, width)), f32((rows, width))],
        [],
        [docs, packed, grad],
        4 * square,
    )
    three = span_of_three(part, where, marks, True, [ended])
    ended, grad_q = call(
        functools.partial(grad_q_kernel, blocks),
        "grads_q",
        [ENDED, bf16((rows, width))],
        [marks],
        [docs, packed, grad, state],
        2 * square,
        after=[three],
    )
    nine = span_of_nine(three, where, marks, True, [ended])
    grad_k, grad_v = call(
        functools.partial(last_kernel, blocks),
        "last",
        [bf16((rows, width)), bf16((rows, width))],
        [where, marks],
        [packed, part_k, part_v, *two_spans(nine, True)],
        4 * rows * width * HEAD_DIM,
    )
    return normed.transpose(1, 0, 2).reshape(tokens, cols), grad_q, grad_k, grad_v


def solution(mesh):
    placed = P(("seq", "head"), None)
    return jax.shard_map(
        on_device,
        mesh=mesh,
        in_specs=(placed, placed, placed, placed, P(), P()),
        out_specs=(placed, P("seq", "head"), P("seq", "head"), P("seq", "head")),
        check_vma=False,
    )
```

```python
import functools

import jax
import jax.numpy as jnp
from jax import lax
from jax.experimental import pallas as pl
from jax.experimental.pallas import tpu as pltpu
from jax.sharding import PartitionSpec as P

HEAD_DIM = 128
TILE = 256


epsilon = 1e-05

F32 = jnp.float32
BF16 = jnp.bfloat16

ROWS = (((0,), (0,)), ((), ()))
FEATURES = (((1,), (1,)), ((), ()))
PLAIN = (((1,), (0,)), ((), ()))


def dot(a, b, dims):
    return lax.dot_general(a, b, dims, preferred_element_type=F32)


def unpacked(packed_ref, at):
    groups, stacked, width = packed_ref.shape
    tokens = stacked // 4
    return packed_ref[:, at * tokens : (at + 1) * tokens, :].reshape(groups * tokens, width)


def head_cols(head):
    return slice(head * HEAD_DIM, (head + 1) * HEAD_DIM)


def meta_kernel(blocks, rows, lengths_ref, where_ref, marks_ref, docs_ref):
    first = where_ref[0] * rows
    last = first + rows - 1

    def clear(i, carry):
        marks_ref[i] = 0
        return carry

    lax.fori_loop(0, 2 * blocks, clear, 0)
    marks_ref[2 * blocks - 1] = 1
    marks_ref[2 * blocks + 1] = 0
    marks_ref[2 * blocks + 3] = rows

    place = first + lax.broadcasted_iota(jnp.int32, (1, rows), 1)

    def step(i, carry):
        begin, start, end = carry
        after = begin + lengths_ref[i]
        marks_ref[begin // rows] = 1
        marks_ref[blocks + jnp.maximum(begin - 1, 0) // rows] = 1

        @pl.when((begin <= first) & (first < after))
        def _():
            marks_ref[2 * blocks] = after - first
            marks_ref[2 * blocks + 1] = jnp.where(begin < first, after - first, 0)

        @pl.when((begin <= last) & (last < after))
        def _():
            marks_ref[2 * blocks + 2] = begin - first
            marks_ref[2 * blocks + 3] = jnp.where(after > last + 1, begin - first, rows)

        inside = (place >= begin) & (place < after)
        return (after, jnp.where(inside, begin, start), jnp.where(inside, after, end))

    zero = jnp.zeros((1, rows), jnp.int32)
    _, start, end = lax.fori_loop(0, lengths_ref.shape[0], step, (jnp.int32(0), zero, zero))
    docs_ref[0:1, :] = start - first
    docs_ref[1:2, :] = end - first


def pack_kernel(*refs):
    _, *arrays, ended_ref, out_ref, held, in_sems, out_sems = refs
    ended_ref[...] = jnp.zeros_like(ended_ref)
    groups, _, width = out_ref.shape
    tokens = arrays[0].shape[0]
    inward = [
        pltpu.make_async_copy(ref, held.at[k], in_sems.at[k]) for k, ref in enumerate(arrays)
    ]
    outward = [
        [
            pltpu.make_async_copy(
                held.at[k, :, pl.ds(at * width, width)],
                out_ref.at[at, pl.ds(k * tokens, tokens), :],
                out_sems.at[k, at],
            )
            for at in range(groups)
        ]
        for k in range(len(arrays))
    ]
    for copy in inward:
        copy.start()
    for copy, parts in zip(inward, outward):
        copy.wait()
        for part in parts:
            part.start()
    for parts in outward:
        for part in parts:
            part.wait()


def parts_kernel(lengths_ref, seq_ref, head_ref, keys_ref, values_ref, ended_ref, out_ref, held, sems):
    copies = [
        pltpu.make_async_copy(ref, held.at[k], sems.at[k])
        for k, ref in enumerate((keys_ref, values_ref))
    ]
    for copy in copies:
        copy.start()
    ended_ref[...] = jnp.zeros_like(ended_ref)
    groups, width, _ = out_ref.shape
    tokens, cols = keys_ref.shape
    last = (seq_ref[0] + 1) * (tokens * groups) - 1
    begin, bound = jnp.int32(0), jnp.int32(0)
    for i in range(lengths_ref.shape[0]):
        bound = jnp.where(begin <= last, begin, bound)
        begin = begin + lengths_ref[i]
    mine = last + 1 - (groups - head_ref[0]) * tokens
    for copy in copies:
        copy.wait()
    place = mine + lax.broadcasted_iota(jnp.int32, (tokens, cols), 0)
    keys = held[0]
    keys = jnp.where(place >= bound, keys, jnp.zeros_like(keys))
    for head in range(cols // HEAD_DIM):
        part = dot(keys[:, head_cols(head)], held[1, :, head_cols(head)], ROWS)
        group, at = divmod(head * HEAD_DIM, width)
        out_ref[group, at : at + HEAD_DIM, :] = part.astype(out_ref.dtype)


def tail_kernel(marks_ref, parts_ref, tail_ref):
    total = parts_ref[0].astype(F32)
    for k in range(1, parts_ref.shape[0]):
        total = total + parts_ref[k].astype(F32)
    tail_ref[...] = total.astype(tail_ref.dtype)


def block_mark(marks_ref, blocks, at, reverse):
    return marks_ref[lax.rem(at + blocks, blocks) + (blocks if reverse else 0)]


def chained(reverse, blocks, where_ref, marks_ref, refs, covers):
    mine, sign = where_ref[0], -1 if reverse else 1
    total = refs[0][...].astype(F32)
    for ref, (low, high) in zip(refs[1:], covers[1:]):
        mark = jnp.int32(0)
        for at in range(low, high + 1):
            mark = jnp.maximum(mark, block_mark(marks_ref, blocks, mine + sign * at, reverse))
        total = jnp.where(mark > 0, 0.0, total) + ref[...].astype(F32)
    return total.astype(BF16)


def three_kernel(reverse, blocks, where_ref, marks_ref, *refs):
    *parts, span_ref = refs
    covers = ((-1, -1), (0, 0), (1, 1))
    span_ref[...] = chained(reverse, blocks, where_ref, marks_ref, parts, covers)


def nine_kernel(reverse, blocks, where_ref, marks_ref, *refs):
    *parts, span_ref = refs
    covers = ((-4, -2), (-1, 1), (2, 4))
    span_ref[...] = chained(reverse, blocks, where_ref, marks_ref, parts, covers)


def entering(reverse, blocks, where_ref, marks_ref, *refs):
    return chained(reverse, blocks, where_ref, marks_ref, refs, ((-18, -10), (-9, -1)))


def intra_kernel(span_ref, packed_ref, intra_ref):
    keys, values, queries = (unpacked(packed_ref, at) for at in range(3))
    rows, width = keys.shape
    for low in range(0, rows, TILE):
        high = low + TILE
        row = low + lax.broadcasted_iota(jnp.int32, (TILE, high), 0)
        column = lax.broadcasted_iota(jnp.int32, (TILE, high), 1)
        mask = (column <= row) & (row < span_ref[1:2, :high])
        for head in range(width // HEAD_DIM):
            cols = head_cols(head)
            scores = dot(queries[low:high, cols], keys[:high, cols], FEATURES)
            attn = jnp.where(mask, scores, 0.0).astype(BF16)
            intra_ref[low:high, cols] = dot(attn, values[:high, cols], PLAIN)


def norm_kernel(blocks, where_ref, marks_ref, packed_ref, intra_ref, gain_ref, *refs):
    far_ref, near_ref, normed_ref, grad_ref, part_ref, state_ref = refs
    queries, cotangent = unpacked(packed_ref, 2), unpacked(packed_ref, 3)
    state = entering(False, blocks, where_ref, marks_ref, far_ref, near_ref)
    state_ref[...] = state
    rows, width = intra_ref.shape
    tile = HEAD_DIM
    for head in range(width // HEAD_DIM):
        cols = head_cols(head)
        at = pl.multiple_of(where_ref[1] * width + head * HEAD_DIM, HEAD_DIM)
        gain = gain_ref[:, pl.ds(at, HEAD_DIM)]
        for low in range(0, rows, tile):
            here = slice(low, low + tile)
            place = low + lax.broadcasted_iota(jnp.int32, (tile, HEAD_DIM), 0)
            inter = dot(queries[here, cols], state[cols, :], PLAIN)
            inter = jnp.where(place < marks_ref[2 * blocks + 1], inter, 0.0)
            attended = intra_ref[here, cols] + inter
            scale = lax.rsqrt(jnp.mean(attended * attended, axis=-1, keepdims=True) + epsilon)
            unit = attended * scale
            normed_ref[here, cols] = (unit * gain).astype(BF16)
            pulled = cotangent[here, cols].astype(F32) * gain
            along = jnp.mean(pulled * unit, axis=-1, keepdims=True)
            grad_ref[here, cols] = (scale * (pulled - unit * along)).astype(BF16)
    place = lax.broadcasted_iota(jnp.int32, (rows, HEAD_DIM), 0)
    in_first = place < marks_ref[2 * blocks]
    for head in range(width // HEAD_DIM):
        cols = head_cols(head)
        q = queries[:, cols]
        kept = jnp.where(in_first, q, jnp.zeros_like(q))
        part_ref[cols, :] = dot(kept, grad_ref[:, cols], ROWS).astype(part_ref.dtype)


def grad_q_kernel(blocks, marks_ref, span_ref, packed_ref, grad_ref, state_ref, ended_ref, grad_q_ref):
    ended_ref[...] = jnp.zeros_like(ended_ref)
    keys, values = unpacked(packed_ref, 0), unpacked(packed_ref, 1)
    rows, width = keys.shape
    for low in range(0, rows, TILE):
        high = low + TILE
        row = low + lax.broadcasted_iota(jnp.int32, (TILE, high), 0)
        column = lax.broadcasted_iota(jnp.int32, (TILE, high), 1)
        mask = (column <= row) & (row < span_ref[1:2, :high])
        place = low + lax.broadcasted_iota(jnp.int32, (TILE, HEAD_DIM), 0)
        carried = place < marks_ref[2 * blocks + 1]
        for head in range(width // HEAD_DIM):
            cols = head_cols(head)
            grad = grad_ref[low:high, cols]
            scores = dot(grad, values[:high, cols], FEATURES)
            grad_attn = jnp.where(mask, scores, 0.0).astype(BF16)
            inter = dot(grad, state_ref[cols, :], FEATURES)
            grad_q = dot(grad_attn, keys[:high, cols], PLAIN) + jnp.where(carried, inter, 0.0)
            grad_q_ref[low:high, cols] = grad_q.astype(BF16)


def turned_kernel(docs_ref, left_ref, right_ref, rows_ref, part_ref):
    left, right, summed = (
        unpacked(*field) if isinstance(field, tuple) else field for field in (left_ref, right_ref, rows_ref)
    )
    rows, width = part_ref.shape
    for low in range(0, rows, TILE):
        high = low + TILE
        row = low + lax.broadcasted_iota(jnp.int32, (TILE, rows - low), 0)
        column = low + lax.broadcasted_iota(jnp.int32, (TILE, rows - low), 1)
        mask = (row <= column) & (row >= docs_ref[0:1, low:])
        for head in range(width // HEAD_DIM):
            cols = head_cols(head)
            turned = dot(left[low:high, cols], right[low:, cols], FEATURES)
            turned = jnp.where(mask, turned, 0.0).astype(BF16)
            part_ref[low:high, cols] = dot(turned, summed[low:, cols], PLAIN)


def grad_k_kernel(docs_ref, packed_ref, grad_ref, ended_ref, part_ref):
    ended_ref[...] = jnp.zeros_like(ended_ref)
    turned_kernel(docs_ref, (packed_ref, 1), grad_ref, (packed_ref, 2), part_ref)


def grad_v_kernel(docs_ref, packed_ref, grad_ref, part_ref):
    turned_kernel(docs_ref, (packed_ref, 0), (packed_ref, 2), grad_ref, part_ref)


def last_kernel(
    blocks, where_ref, marks_ref, packed_ref, part_k_ref, part_v_ref, far_ref, near_ref, grad_k_ref, grad_v_ref
):
    keys, values = unpacked(packed_ref, 0), unpacked(packed_ref, 1)
    back = entering(True, blocks, where_ref, marks_ref, far_ref, near_ref)
    rows, width = keys.shape
    place = lax.broadcasted_iota(jnp.int32, (rows, HEAD_DIM), 0)
    later = place >= marks_ref[2 * blocks + 3]
    for head in range(width // HEAD_DIM):
        cols = head_cols(head)
        inter = dot(values[:, cols], back[cols, :], FEATURES)
        grad_k_ref[:, cols] = (part_k_ref[:, cols] + jnp.where(later, inter, 0.0)).astype(BF16)
        inter = dot(keys[:, cols], back[cols, :], PLAIN)
        grad_v_ref[:, cols] = (part_v_ref[:, cols] + jnp.where(later, inter, 0.0)).astype(BF16)


SMEM = pl.BlockSpec(memory_space=pltpu.SMEM)
VMEM = pl.BlockSpec(memory_space=pltpu.VMEM)
ANYWHERE = pl.BlockSpec(memory_space=pl.ANY)
ENDED = jax.ShapeDtypeStruct((8, HEAD_DIM), F32)


def call(
    kernel, name, outs, scalars, arrays, flops, scratch=(), after=(), in_specs=None, out_specs=None, limit=40, aliases=None
):
    moved = sum(a.size * a.dtype.itemsize for a in (*arrays, *outs))
    given = len(scalars) + len(arrays)

    def body(*refs):
        kernel(*refs[:given], *refs[given + len(after) :])

    return pl.pallas_call(
        body,
        name=name,
        out_shape=outs,
        in_specs=[SMEM] * len(scalars) + (in_specs or [VMEM] * len(arrays)) + [ANYWHERE] * len(after),
        out_specs=out_specs or [VMEM] * len(outs),
        scratch_shapes=list(scratch),
        input_output_aliases=aliases or {},
        compiler_params=pltpu.CompilerParams(vmem_limit_bytes=limit * 1024 * 1024),
        cost_estimate=pl.CostEstimate(flops=flops, bytes_accessed=moved, transcendentals=0),
    )(*scalars, *arrays, *after)


def across_head(parts):
    return lax.all_to_all(parts, "head", split_axis=0, concat_axis=0, tiled=True)


def to_heads(arrays, marks):
    groups, count = lax.axis_size("head"), len(arrays)
    tokens, cols = arrays[0].shape
    ended, packed = call(
        pack_kernel,
        "pack",
        [ENDED, jax.ShapeDtypeStruct((groups, count * tokens, cols // groups), BF16)],
        [marks],
        arrays,
        0,
        [
            pltpu.VMEM((count, tokens, cols), BF16),
            pltpu.SemaphoreType.DMA((count,)),
            pltpu.SemaphoreType.DMA((count, groups)),
        ],
        (),
        [ANYWHERE] * count,
        [VMEM, ANYWHERE],
        60,
    )
    return ended, packed


def from_block(field, step, reach, reverse):
    blocks = lax.axis_size("seq")
    pairs = []
    for at in range(blocks):
        to = at + step
        if to < blocks or to - blocks - step + reach >= 0:
            pairs.append((at, to % blocks))
    if reverse:
        pairs = [(blocks - 1 - at, blocks - 1 - to) for at, to in pairs]
    return lax.ppermute(field, "seq", pairs)


def span(kernel, parts, where, marks, reverse, after=()):
    blocks = lax.axis_size("seq")
    return call(
        functools.partial(kernel, reverse, blocks),
        kernel.__name__.replace("kernel", "back" if reverse else "forward"),
        [jax.ShapeDtypeStruct(parts[0].shape, BF16)],
        [where, marks],
        parts,
        len(parts) * parts[0].size,
        after=after,
    )[0]


def span_of_three(part, where, marks, reverse, after=()):
    parts = [from_block(part, 1, 0, reverse), part, from_block(part, -1, 0, reverse)]
    return span(three_kernel, parts, where, marks, reverse, after)


def span_of_nine(three, where, marks, reverse, after=()):
    parts = [from_block(three, 3, 1, reverse), three, from_block(three, -3, 1, reverse)]
    return span(nine_kernel, parts, where, marks, reverse, after)


def two_spans(nine, reverse):
    return [from_block(nine, 14, 4, reverse), from_block(nine, 5, 4, reverse)]


def on_device(queries, keys, values, cotangent, gain, lengths):
    groups, blocks = lax.axis_size("head"), lax.axis_size("seq")
    tokens, cols = queries.shape
    rows, width = tokens * groups, cols // groups
    square = rows * rows * width
    here = lax.axis_index("head").astype(jnp.int32)
    where = jnp.stack([lax.axis_index("seq").astype(jnp.int32), here])
    f32 = functools.partial(jax.ShapeDtypeStruct, dtype=F32)
    bf16 = functools.partial(jax.ShapeDtypeStruct, dtype=BF16)
    int32 = functools.partial(jax.ShapeDtypeStruct, dtype=jnp.int32)
    started, parts = call(
        parts_kernel,
        "parts",
        [ENDED, bf16((groups, width, HEAD_DIM))],
        [lengths, lax.axis_index("seq").astype(jnp.int32).reshape(1), here.reshape(1)],
        [keys, values],
        2 * tokens * cols * HEAD_DIM,
        [
            pltpu.VMEM((2, tokens, cols), BF16),
            pltpu.SemaphoreType.DMA((2,)),
        ],
        in_specs=[ANYWHERE] * 2,
        limit=60,
    )
    marks, docs = call(
        functools.partial(meta_kernel, blocks, rows),
        "meta",
        [int32((2 * blocks + 4,)), int32((2, rows))],
        [lengths, where],
        [],
        rows,
        after=[started],
        out_specs=[SMEM, VMEM],
    )
    gathered = across_head(parts)
    ended, packed = to_heads([keys, values, queries, cotangent], marks)
    (tail,) = call(
        tail_kernel,
        "tail",
        [bf16((width, HEAD_DIM))],
        [marks],
        [gathered],
        gathered.size,
        after=[ended],
    )
    packed = across_head(packed)
    three = span_of_three(tail, where, marks, False)
    before = two_spans(span_of_nine(three, where, marks, False), False)
    (inside,) = call(intra_kernel, "intra", [f32((rows, width))], [], [docs, packed], 2 * square)
    normed, grad, part, state = call(
        functools.partial(norm_kernel, blocks),
        "norm",
        [bf16((rows, width)), bf16((rows, width)), bf16((width, HEAD_DIM)), bf16((width, HEAD_DIM))],
        [where, marks],
        [packed, inside, gain.reshape(1, cols), *before],
        4 * rows * width * HEAD_DIM,
    )

    normed = across_head(normed.reshape(groups, tokens, width))
    ended, part_k = call(
        grad_k_kernel, "grads_k", [ENDED, f32((rows, width))], [], [docs, packed, grad], 2 * square
    )
    three = span_of_three(part, where, marks, True, [ended])
    ended, grad_q = call(
        functools.partial(grad_q_kernel, blocks),
        "grads_q",
        [ENDED, bf16((rows, width))],
        [marks],
        [docs, packed, grad, state],
        2 * square,
        after=[three],
    )
    nine = span_of_nine(three, where, marks, True, [ended])
    (part_v,) = call(
        grad_v_kernel, "grads_v", [f32((rows, width))], [], [docs, packed, grad], 2 * square, after=[nine]
    )
    grad_k, grad_v = call(
        functools.partial(last_kernel, blocks),
        "last",
        [bf16((rows, width)), bf16((rows, width))],
        [where, marks],
        [packed, part_k, part_v, *two_spans(nine, True)],
        4 * rows * width * HEAD_DIM,
    )
    return normed.transpose(1, 0, 2).reshape(tokens, cols), grad_q, grad_k, grad_v


def solution(mesh):
    placed = P(("seq", "head"), None)
    return jax.shard_map(
        on_device,
        mesh=mesh,
        in_specs=(placed, placed, placed, placed, P(), P()),
        out_specs=(placed, P("seq", "head"), P("seq", "head"), P("seq", "head")),
        check_vma=False,
    )
```
